32 devices in a mesh: row: 4 (over y, core), col: 8 (over z, x).
Axes of the slice: x: 2, y: 2, z: 4, core: 2. Of those that a mesh axis runs over, the one named last changes fastest.
Arguments:
- field: float32 [32, 128, 4096], P(None, 'row', 'col'), may hold values from -4 to 4
- right_side: float32 [32, 128, 4096], P(None, 'row', 'col'), may hold values from -6 to 6
- kappa: float32 [128, 4096], P('row', 'col'), may hold values from 0.1 to 3
- fronts: bfloat16 [5, 2048, 4096], P(None, 'row', 'col'), may hold values from -2 to 2
Outputs:
- residual: float32 [32, 128, 4096], P(None, 'row', 'col')
- separator_solution: float32 [128, 4096], P('row', 'col')
The draws below stay inside these ranges and needn't reach their ends.
All inputs are finite; a program needn't handle non-finite values.
Results may differ from the reference program's by a relative error of at most 0.022.
Values sent between devices are 32-bit elements; how exact they have to be, the bound alone decides.
No kernel may reach another device: no remote copies, remote signals or barrier semaphores. Data moves between devices by JAX's collectives and lax.ppermute only.
A program may use at most 64 MiB of HBM per device.

```python
import math
import jax
import jax.numpy as jnp
from jax import lax

K = 32
SEP = 512
CR = 32
COL_BITS = 3
LEVELS = 5
NR = 128
NC = 4096
FR = 2048
N_ROW = 4
N_COL = 8


def draw_fronts(key, part):
    shape = (LEVELS, FR, NC)
    noise = jnp.clip(jax.random.normal(key, shape, jnp.float32), -4.0, 4.0)
    noise = noise * (0.4 / math.sqrt(SEP))
    row_idx = jnp.arange(FR, dtype=jnp.int32)[None, :, None]
    col_idx = jnp.arange(NC, dtype=jnp.int32)[None, None, :]
    diagonal = row_idx % SEP == col_idx % SEP
    return (noise + jnp.where(diagonal, 0.7, 0.0)).astype(jnp.bfloat16)


def block_levels(stream_key, extent, pieces, least, top_value):
    loudness = 1.0
    for axis_at, shards_of in pieces:
        heights = jax.random.uniform(jax.random.fold_in(jax.random.fold_in(stream_key, 6), axis_at), (shards_of,), jnp.float32, least / len(pieces), top_value / len(pieces))
        loudness = loudness * jnp.repeat(jnp.exp(heights), extent[axis_at] // shards_of).reshape((-1,) + (1,) * (len(extent) - 1 - axis_at))
    return loudness


def bell_draw(key, shape, deviation, bound, split=(), kind=jnp.bfloat16):
    loudness = block_levels(key, shape, split, -0.22, 0.18) if split else 1.0
    values = jax.random.normal(key, shape, jnp.float32) * deviation * loudness
    return jnp.minimum(jnp.maximum(values, -bound), bound).astype(kind)


def setup_inputs(seed: int = 0) -> dict:
    key_of = jax.random.split(jax.random.key(seed), 5)
    return {
        "field": bell_draw(key_of[0], (K, NR, NC), 0.5, 4.0, ((1, 4), (2, 8)), jnp.float32),
        "right_side": bell_draw(key_of[1], (K, NR, NC), 1.0, 6.0, ((1, 4), (2, 8)), jnp.float32),
        "kappa": jnp.clip(jnp.exp(math.log(3.0) - 3.4011974 * jax.random.uniform(key_of[2], (NR, NC), jnp.float32) ** block_levels(key_of[2], (NR, NC), ((0, 4), (1, 8)), -0.2, 0.2)), 0.1, 3.0),
        "fronts": draw_fronts(jax.random.fold_in(key_of[4], 71), 0),
    }


def rounded(value):
    return lax.optimization_barrier(value.astype(jnp.bfloat16)).astype(jnp.float32)


def level_setup(level):
    rows_idx = jnp.arange(N_ROW, dtype=jnp.int32)
    cols_idx = jnp.arange(N_COL, dtype=jnp.int32)
    if level < COL_BITS:
        lower = jnp.bitwise_and(jnp.right_shift(cols_idx, level), 1) == 0
        lower = jnp.broadcast_to(lower[None, :], (N_ROW, N_COL))
        partner = jnp.bitwise_xor(cols_idx, 1 << level).astype(jnp.int32)
        axis_pick = 1
    else:
        shift_by = level - COL_BITS
        lower = jnp.bitwise_and(jnp.right_shift(rows_idx, shift_by), 1) == 0
        lower = jnp.broadcast_to(lower[:, None], (N_ROW, N_COL))
        partner = jnp.bitwise_xor(rows_idx, 1 << shift_by).astype(jnp.int32)
        axis_pick = 0
    return lower[:, :, None, None], partner, axis_pick


def reference(field, right_side, kappa, fronts):
    padded = jnp.pad(field, ((0, 0), (1, 1), (1, 1)))
    near = padded[:, 2:, 1:-1] + padded[:, :-2, 1:-1] + padded[:, 1:-1, 2:] + padded[:, 1:-1, :-2]
    residual = right_side - ((4.0 + kappa) * field - near)
    edge = residual[:, CR - 1::CR, :]
    state = edge.reshape(K, N_ROW, N_COL, SEP).transpose(1, 2, 0, 3)
    for level in range(LEVELS):
        lower, partner, axis_pick = level_setup(level)
        front = fronts[level].reshape(N_ROW, SEP, N_COL, SEP).astype(jnp.float32)
        first = jnp.einsum('rcka,racb->rckb', rounded(state), front)
        got = jnp.take(first, partner, axis=axis_pick)
        state = jnp.where(lower, first + got, got - first)
    for level in range(LEVELS - 1, -1, -1):
        lower, partner, axis_pick = level_setup(level)
        front = fronts[level].reshape(N_ROW, SEP, N_COL, SEP).astype(jnp.float32)
        got = jnp.take(state, partner, axis=axis_pick)
        combined = jnp.where(lower, state - got, state + got)
        state = jnp.einsum('rcka,rbca->rckb', rounded(combined), front)
    separator_solution = state.transpose(0, 2, 1, 3).reshape(N_ROW * K, N_COL * SEP)
    return residual, separator_solution
```

```python
import functools

import jax
import jax.numpy as jnp
from jax import lax
from jax.experimental import pallas as pl
from jax.experimental.pallas import tpu as pltpu
from jax.sharding import PartitionSpec as P

F32 = jnp.float32
BF16 = jnp.bfloat16


def grid_pairs(rows, cols, target):
    pairs = []
    for i in range(rows):
        for j in range(cols):
            to_i, to_j = target(i, j)
            pairs.append((i * cols + j, to_i * cols + to_j))
    assert len({to for _, to in pairs}) == rows * cols
    return pairs


def swapped(value, axis, bit):
    count = lax.axis_size(axis)
    return lax.ppermute(value, axis, [(s, s ^ (1 << bit)) for s in range(count)])


def rotated(value, axis, step):
    count = lax.axis_size(axis)
    return lax.ppermute(value, axis, [(s, (s + step) % count) for s in range(count)])


def times_front(value, front):
    return jnp.dot(value.astype(BF16), front, preferred_element_type=F32)


def times_front_t(value, front):
    return lax.dot_general(
        value.astype(BF16), front, (((1,), (1,)), ((), ())), preferred_element_type=F32
    )


def stencil_kernel(field, right, kappa, above, below, left, right_col, out):
    rows, width = field.shape[1:]
    row = lax.broadcasted_iota(jnp.int32, (rows, width), 0)
    lane = lax.broadcasted_iota(jnp.int32, (rows, width), 1)
    eye_row = lax.broadcasted_iota(jnp.int32, (rows, rows), 0)
    eye = eye_row == lax.broadcasted_iota(jnp.int32, (rows, rows), 1)
    centre = 4.0 + kappa[...]
    for k in range(field.shape[0]):
        f = field[k]
        up = jnp.where(row == 0, above[pl.ds(k, 1), :], pltpu.roll(f, 1, 0))
        down = jnp.where(row == rows - 1, below[pl.ds(k, 1), :], pltpu.roll(f, rows - 1, 0))
        west = jnp.sum(jnp.where(eye, left[pl.ds(k, 1), :], 0.0), axis=1, keepdims=True)
        east = jnp.sum(jnp.where(eye, right_col[pl.ds(k, 1), :], 0.0), axis=1, keepdims=True)
        before = jnp.where(lane == 0, west, pltpu.roll(f, 1, 1))
        after = jnp.where(lane == width - 1, east, pltpu.roll(f, width - 1, 1))
        out[k] = right[k] - (centre * f - (down + up + after + before))


def stencil(field, right_side, kappa, above, below, left, right, block):
    count, rows, width = field.shape
    cube = pl.BlockSpec((block, rows, width), lambda k: (k, 0, 0))
    line = pl.BlockSpec((block, width), lambda k: (k, 0))
    side = pl.BlockSpec((block, rows), lambda k: (k, 0))
    return pl.pallas_call(
        stencil_kernel,
        grid=(count // block,),
        in_specs=[cube, cube, pl.BlockSpec((rows, width), lambda k: (0, 0)), line, line, side, side],
        out_specs=cube,
        out_shape=jax.ShapeDtypeStruct(field.shape, F32),
        cost_estimate=pl.CostEstimate(
            flops=8 * field.size, bytes_accessed=12 * field.size, transcendentals=0
        ),
    )(field, right_side, kappa, above, below, left, right)


def body(field, right_side, kappa, fronts):
    rows, cols = lax.axis_size("row"), lax.axis_size("col")
    i, j = lax.axis_index("row"), lax.axis_index("col")
    col_bits, row_bits = cols.bit_length() - 1, rows.bit_length() - 1
    odd = j % 2 == 1

    below = rotated(field[:, 0, :], "row", -1)
    below = jnp.where(i == rows - 1, 0.0, below)
    above = rotated(field[:, -1, :], "row", 1)
    above = jnp.where(i == 0, 0.0, above)

    first, last = field[:, :, 0], field[:, :, -1]
    near_side = lax.ppermute(
        jnp.where(odd, first, last), "col", [(s, s ^ 1) for s in range(cols)]
    )

    def beyond(r, c):
        if c in (0, cols - 1):
            return r ^ 1, c
        return r, c + 1 if c % 2 else c - 1

    far_side = lax.ppermute(
        jnp.where(odd, last, first), ("row", "col"), grid_pairs(rows, cols, beyond)
    )
    far_side = jnp.where((j == 0) | (j == cols - 1), 0.0, far_side)
    left = jnp.where(odd, near_side, far_side)
    right = jnp.where(odd, far_side, near_side)

    edge = field[:, -1, :]
    before = jnp.concatenate([left[:, -1:], edge[:, :-1]], axis=1)
    after = jnp.concatenate([edge[:, 1:], right[:, -1:]], axis=1)
    near = below + field[:, -2, :] + after + before
    state = right_side[:, -1, :] - ((4.0 + kappa[-1]) * edge - near)

    places = [("col", b, j) for b in range(col_bits)] + [("row", b, i) for b in range(row_bits)]
    for level, (axis, bit, owner) in enumerate(places):
        lower = jnp.bitwise_and(jnp.right_shift(owner, bit), 1) == 0
        first_product = times_front(state, fronts[level])
        got = swapped(first_product, axis, bit)
        if level + 1 < len(places):
            state = jnp.where(lower, first_product + got, got - first_product)
        else:
            state = times_front_t(got + got, fronts[level])
    for level in range(len(places) - 2, -1, -1):
        axis, bit, owner = places[level]
        lower = jnp.bitwise_and(jnp.right_shift(owner, bit), 1) == 0
        got = swapped(state, axis, bit)
        state = times_front_t(jnp.where(lower, state - got, state + got), fronts[level])

    residual = stencil(field, right_side, kappa, above, below, left, right, 8)
    return residual, state


def solution(mesh):
    placed = (P(None, "row", "col"), P(None, "row", "col"), P("row", "col"), P(None, "row", "col"))
    return jax.shard_map(
        body,
        mesh=mesh,
        in_specs=placed,
        out_specs=(P(None, "row", "col"), P("row", "col")),
        check_vma=False,
    )
```

```python
import functools

import jax
import jax.numpy as jnp
from jax import lax
from jax.experimental import pallas as pl
from jax.experimental.pallas import tpu as pltpu
from jax.sharding import PartitionSpec as P

F32 = jnp.float32
BF16 = jnp.bfloat16
TILE = 8
LANES = 128
ODD, HAS_BELOW, HAS_OUTER, SIGN = 0, 1, 2, 3
NEAR_FRONT, FAR_FRONT, NEAR_SIDE, FAR_SIDE = 0, 1, 2, 3


def swapped(value, axis, bit):
    count = lax.axis_size(axis)
    return lax.ppermute(value, axis, [(s, s ^ (1 << bit)) for s in range(count)])


def rotated(value, axis, step):
    count = lax.axis_size(axis)
    return lax.ppermute(value, axis, [(s, (s + step) % count) for s in range(count)])


def outer_sides(value, cols):
    def target(c):
        return c - 2 + 4 * (c % 2) if 0 <= c - 2 + 4 * (c % 2) < cols else c ^ 1

    return lax.ppermute(value, "col", [(c, target(c)) for c in range(cols)])


def beyond_sides(value, rows, cols):
    pairs = []
    for r in range(rows):
        for c in range(cols):
            to = (r ^ 1, c) if c in (0, cols - 1) else (r, c + 1 if c % 2 else c - 1)
            pairs.append((r * cols + c, to[0] * cols + to[1]))
    return lax.ppermute(value, ("row", "col"), pairs)


def times_front(value, front):
    return jnp.dot(value.astype(BF16), front, preferred_element_type=F32)


def times_front_t(value, front):
    return lax.dot_general(
        value.astype(BF16), front, (((1,), (1,)), ((), ())), preferred_element_type=F32
    )


def in_vmem(shape):
    return pltpu.VMEM(shape, F32)


VMEM = pl.BlockSpec(memory_space=pltpu.VMEM)
SMALL = pltpu.CompilerParams(vmem_limit_bytes=4 * 2**20)


def interface_kernel(top, bottom, right, kappa, switches, first_row, part, sides):
    count, _, width = top.shape
    lane = lax.broadcasted_iota(jnp.int32, (count, width), 1)
    first_row[...] = top[:, 0, :]
    edge = bottom[:, TILE - 1, :]
    before = jnp.where(lane == 0, 0.0, pltpu.roll(edge, 1, 1))
    after = jnp.where(lane == width - 1, 0.0, pltpu.roll(edge, width - 1, 1))
    near = bottom[:, TILE - 2, :] + after + before
    part[...] = right[:, TILE - 1, :] - ((4.0 + kappa[TILE - 1 :, :]) * edge - near)
    odd = switches[ODD : ODD + 1, :1] > 0.0
    west, east = edge[:, :1], edge[:, width - 1 :]
    shape = (count, LANES)
    eye = lax.broadcasted_iota(jnp.int32, shape, 0) == lax.broadcasted_iota(jnp.int32, shape, 1)
    near_side = jnp.sum(jnp.where(eye, jnp.where(odd, west, east), 0.0), axis=0, keepdims=True)
    far_side = jnp.sum(jnp.where(eye, jnp.where(odd, east, west), 0.0), axis=0, keepdims=True)
    row = lax.broadcasted_iota(jnp.int32, (TILE, LANES), 0)
    sides[...] = jnp.where(row == NEAR_SIDE, near_side, jnp.where(row == FAR_SIDE, far_side, 0.0))


def interface(field, right_side, kappa, switches):
    count, rows, width = field.shape
    last = rows // TILE - 1
    strip = (count, TILE, width)
    return pl.pallas_call(
        interface_kernel,
        grid=(1,),
        in_specs=[
            pl.BlockSpec(strip, lambda _: (0, 0, 0)),
            pl.BlockSpec(strip, lambda _: (0, last, 0)),
            pl.BlockSpec(strip, lambda _: (0, last, 0)),
            pl.BlockSpec((TILE, width), lambda _: (last, 0)),
            VMEM,
        ],
        out_specs=[VMEM] * 3,
        out_shape=[in_vmem((count, width)), in_vmem((count, width)), in_vmem((TILE, LANES))],
    )(field, field, right_side, kappa, switches)


def first_product_kernel(part, below, sides, outer, fronts, switches, message):
    count, width = part.shape
    state = part[...] + switches[HAS_BELOW : HAS_BELOW + 1, :1] * below[...]
    message[:count, :] = jnp.dot(state.astype(BF16), fronts[0], preferred_element_type=F32)
    odd = switches[ODD : ODD + 1, :1] > 0.0
    top = fronts[0, :16, :].astype(F32)[:1]
    bottom = fronts[0, width - 16 :, :].astype(F32)[15:]
    row = lax.broadcasted_iota(jnp.int32, (TILE, width), 0)
    ends = jnp.where(
        row == NEAR_FRONT,
        jnp.where(odd, top, bottom),
        jnp.where(row == FAR_FRONT, jnp.where(odd, bottom, top), 0.0),
    )
    message[count:, :] = ends
    row = lax.broadcasted_iota(jnp.int32, (TILE, LANES), 0)
    given = switches[HAS_OUTER : HAS_OUTER + 1, :1] * outer[FAR_SIDE : FAR_SIDE + 1, :]
    columns = jnp.where(row == NEAR_SIDE, sides[...], jnp.where(row == FAR_SIDE, given, 0.0))
    message[count:, :LANES] = ends[:, :LANES] + columns


def first_product(part, below, sides, outer, fronts, switches):
    count, width = part.shape
    return pl.pallas_call(
        first_product_kernel,
        in_specs=[VMEM] * 6,
        out_specs=VMEM,
        out_shape=in_vmem((count + TILE, width)),
        compiler_params=SMALL,
    )(part, below, sides, outer, fronts, switches)


def second_product_kernel(mine, theirs, fronts, switches, out):
    count, width = out.shape
    sign = switches[SIGN : SIGN + 1, :1]
    row = lax.broadcasted_iota(jnp.int32, (TILE, width), 0)
    my_rows, their_rows = mine[count:, :], theirs[count:, :]
    ends = jnp.where(row < 2, my_rows, jnp.where(row < 4, pltpu.roll(their_rows, 2, 0), 0.0))
    row = row[:, :LANES]
    columns = jnp.where(
        row < 2,
        sign * pltpu.roll(their_rows[:, :LANES], TILE - 2, 0),
        jnp.where(row < 4, my_rows[:, :LANES], 0.0),
    )
    missing = lax.dot_general(
        columns[:, :count].astype(BF16),
        ends.astype(BF16),
        (((0,), (0,)), ((), ())),
        preferred_element_type=F32,
    )
    state = sign * mine[:count, :] + theirs[:count, :] + missing
    out[...] = jnp.dot(state.astype(BF16), fronts[1], preferred_element_type=F32)


def second_product(mine, theirs, fronts, switches):
    count, width = mine.shape[0] - TILE, mine.shape[1]
    return pl.pallas_call(
        second_product_kernel,
        in_specs=[VMEM] * 4,
        out_specs=VMEM,
        out_shape=in_vmem((count, width)),
        compiler_params=SMALL,
    )(mine, theirs, fronts, switches)


def stencil_kernel(field, right, kappa, above, below, left, right_col, *rest):
    out = rest[-1]
    rows, width = field.shape[1:]
    row = lax.broadcasted_iota(jnp.int32, (rows, width), 0)
    lane = lax.broadcasted_iota(jnp.int32, (rows, width), 1)
    eye_row = lax.broadcasted_iota(jnp.int32, (rows, rows), 0)
    eye = eye_row == lax.broadcasted_iota(jnp.int32, (rows, rows), 1)
    centre = 4.0 + kappa[...]
    for k in range(field.shape[0]):
        f = field[k]
        up = jnp.where(row == 0, above[pl.ds(k, 1), :], pltpu.roll(f, 1, 0))
        down = jnp.where(row == rows - 1, below[pl.ds(k, 1), :], pltpu.roll(f, rows - 1, 0))
        west = jnp.sum(jnp.where(eye, left[pl.ds(k, 1), :], 0.0), axis=1, keepdims=True)
        east = jnp.sum(jnp.where(eye, right_col[pl.ds(k, 1), :], 0.0), axis=1, keepdims=True)
        before = jnp.where(lane == 0, west, pltpu.roll(f, 1, 1))
        after = jnp.where(lane == width - 1, east, pltpu.roll(f, width - 1, 1))
        out[k] = right[k] - (centre * f - (down + up + after + before))


def stencil(arrays, done, first, blocks, block):
    field = arrays[0]
    count, rows, width = field.shape
    cube = pl.BlockSpec((block, rows, width), lambda k: (first + k, 0, 0))
    line = pl.BlockSpec((block, width), lambda k: (first + k, 0))
    side = pl.BlockSpec((block, rows), lambda k: (first + k, 0))
    specs = [cube, cube, pl.BlockSpec((rows, width), lambda k: (0, 0)), line, line, side, side]
    part = blocks * block * rows * width
    if done is not None:
        arrays = (*arrays, done)
        specs = [*specs, pl.BlockSpec(memory_space=pl.ANY)]
    return pl.pallas_call(
        stencil_kernel,
        grid=(blocks,),
        in_specs=specs,
        out_specs=cube,
        out_shape=jax.ShapeDtypeStruct(field.shape, F32),
        input_output_aliases={} if done is None else {7: 0},
        cost_estimate=pl.CostEstimate(flops=8 * part, bytes_accessed=12 * part, transcendentals=0),
    )(*arrays)


def tied(*values):
    return lax.optimization_barrier(values)


def body(field, right_side, kappa, fronts):
    rows, cols = lax.axis_size("row"), lax.axis_size("col")
    i, j = lax.axis_index("row"), lax.axis_index("col")
    col_bits, row_bits = cols.bit_length() - 1, rows.bit_length() - 1
    odd = j % 2 == 1
    outer_at = jnp.where(odd, j - 2, j + 2)
    has_outer = (outer_at >= 0) & (outer_at < cols)
    values = [odd, i < rows - 1, has_outer, jnp.where(odd, -1.0, 1.0)]
    values = jnp.stack([v.astype(F32) for v in values] + [jnp.zeros((), F32)] * (TILE - len(values)))
    switches = jnp.broadcast_to(values[:, None], (TILE, LANES))

    first_row, part, sides = interface(field, right_side, kappa, switches)
    below = rotated(first_row, "row", -1)
    outer = outer_sides(sides, cols)
    product = first_product(part, below, sides, outer, fronts, switches)
    got = swapped(product, "col", 0)
    product = second_product(product, got, fronts, switches)

    places = [("col", b, j) for b in range(col_bits)] + [("row", b, i) for b in range(row_bits)]
    top = len(places) - 1
    for level in range(1, top + 1):
        axis, bit, owner = places[level]
        lower = jnp.bitwise_and(jnp.right_shift(owner, bit), 1) == 0
        got = swapped(product, axis, bit)
        if level < top:
            state = jnp.where(lower, product + got, got - product)
            product = times_front(state, fronts[level + 1])
        else:
            state = times_front_t(got + got, fronts[level])

    below = jnp.where(i == rows - 1, 0.0, below)
    above = jnp.where(i == 0, 0.0, rotated(field[:, -1, :], "row", 1))
    west, east = field[:, :, 0], field[:, :, -1]
    near_side = swapped(jnp.where(odd, west, east), "col", 0)
    far_side = beyond_sides(jnp.where(odd, east, west), rows, cols)
    far_side = jnp.where((j == 0) | (j == cols - 1), 0.0, far_side)
    left = jnp.where(odd, near_side, far_side)
    right = jnp.where(odd, far_side, near_side)
    arrays = (field, right_side, kappa, above, below, left, right)

    residual, at = None, 0
    shares = {2: 1, 1: 1, 0: 2}
    for level in range(top - 1, -1, -1):
        axis, bit, owner = places[level]
        lower = jnp.bitwise_and(jnp.right_shift(owner, bit), 1) == 0
        if level in shares:
            state, *arrays = tied(state, *arrays)
        got = swapped(state, axis, bit)
        if level in shares:
            residual = stencil(tuple(arrays), residual, at, shares[level], TILE)
            at += shares[level]
            got, residual = tied(got, residual)
        state = times_front_t(jnp.where(lower, state - got, state + got), fronts[level])
    return residual, state


def solution(mesh):
    placed = (P(None, "row", "col"), P(None, "row", "col"), P("row", "col"), P(None, "row", "col"))
    return jax.shard_map(
        body,
        mesh=mesh,
        in_specs=placed,
        out_specs=(P(None, "row", "col"), P("row", "col")),
        check_vma=False,
    )
```

```python
import functools

import jax
import jax.numpy as jnp
from jax import lax
from jax.experimental import pallas as pl
from jax.experimental.pallas import tpu as pltpu
from jax.sharding import PartitionSpec as P

F32 = jnp.float32
BF16 = jnp.bfloat16
TILE = 8
LANES = 128
ODD, HAS_ABOVE, HAS_BELOW, HAS_OUTER, SIGN = 0, 1, 2, 3, 4
NEAR_FRONT, FAR_FRONT = 0, 1


def swapped(value, axis, bit):
    count = lax.axis_size(axis)
    return lax.ppermute(value, axis, [(s, s ^ (1 << bit)) for s in range(count)])


def rotated(value, axis, step):
    count = lax.axis_size(axis)
    return lax.ppermute(value, axis, [(s, (s + step) % count) for s in range(count)])


def outer_sides(value, cols):
    def target(c):
        return c - 2 + 4 * (c % 2) if 0 <= c - 2 + 4 * (c % 2) < cols else c ^ 1

    return lax.ppermute(value, "col", [(c, target(c)) for c in range(cols)])


def times_front(value, front):
    return jnp.dot(value.astype(BF16), front, preferred_element_type=F32)


def times_front_t(value, front):
    return lax.dot_general(
        value.astype(BF16), front, (((1,), (1,)), ((), ())), preferred_element_type=F32
    )


def in_vmem(shape):
    return pltpu.VMEM(shape, F32)


def in_hbm(value):
    return pltpu.with_memory_space_constraint(value, pltpu.HBM)


VMEM = pl.BlockSpec(memory_space=pltpu.VMEM)
HBM = pl.BlockSpec(memory_space=pltpu.HBM)
SMALL = pltpu.CompilerParams(vmem_limit_bytes=6 * 2**20)


def interface_kernel(field, right, kappa, first_row, last_row, part, rim, f, ahead, k8, f_sems, sems):
    count, rows, width = f.shape
    strip = pl.ds(rows - TILE, TILE)
    pieces = [pl.ds(at, TILE) for at in range(0, count, TILE)]
    fields = [
        pltpu.make_async_copy(field.at[here], f.at[here], f_sems.at[p])
        for p, here in enumerate(pieces)
    ]
    others = [
        pltpu.make_async_copy(right.at[:, strip, :], ahead, sems.at[0]),
        pltpu.make_async_copy(kappa.at[strip, :], k8, sems.at[1]),
    ]
    for copy in (*fields, *others):
        copy.start()
    row = lax.broadcasted_iota(jnp.int32, (rows, LANES), 0)
    lane = lax.broadcasted_iota(jnp.int32, (rows, LANES), 1)
    column = lax.broadcasted_iota(jnp.int32, (TILE, width), 1)
    for copy, here in zip(fields, pieces):
        copy.wait()
        first_row[here, :] = f[here, 0, :]
        edge = f[here, rows - 1, :]
        last_row[here, :] = edge
        before = jnp.where(column == 0, 0.0, pltpu.roll(edge, 1, 1))
        after = jnp.where(column == width - 1, 0.0, pltpu.roll(edge, width - 1, 1))
        part[here, :] = f[here, rows - 2, :] + after + before
        for k in range(here.start, here.start + TILE):
            first, last = f[k, :, :1], f[k, :, width - 1 :]
            spread = jnp.where(lane == row, first, jnp.where(lane == row + rows, last, 0.0))
            rim[k : k + 1, :] = jnp.sum(spread, axis=0, keepdims=True)
    for copy in others:
        copy.wait()
    centre = 4.0 + k8[TILE - 1 :, :]
    part[...] = ahead[:, TILE - 1, :] - (centre * last_row[...] - part[...])


def interface(field, right_side, kappa):
    count, _, width = field.shape
    line = in_vmem((count, width))
    return pl.pallas_call(
        interface_kernel,
        in_specs=[HBM] * 3,
        out_specs=[VMEM] * 4,
        out_shape=[line, line, line, in_vmem((count, LANES))],
        scratch_shapes=[
            pltpu.VMEM(field.shape, F32),
            pltpu.VMEM((count, TILE, width), F32),
            pltpu.VMEM((TILE, width), F32),
            pltpu.SemaphoreType.DMA((count // TILE,)),
            pltpu.SemaphoreType.DMA((2,)),
        ],
        compiler_params=SMALL,
    )(in_hbm(field), in_hbm(right_side), in_hbm(kappa))


def first_product_kernel(part, below, rim, outer, fronts, switches, message):
    count, width = part.shape
    rows = LANES // 4
    state = part[...] + switches[HAS_BELOW : HAS_BELOW + 1, :1] * below[...]
    message[:count, :] = jnp.dot(state.astype(BF16), fronts[0], preferred_element_type=F32)
    odd = switches[ODD : ODD + 1, :1] > 0.0
    top = fronts[0, :16, :].astype(F32)[:1]
    bottom = fronts[0, width - 16 :, :].astype(F32)[15:]
    row = lax.broadcasted_iota(jnp.int32, (TILE, width), 0)
    message[count : count + TILE, :] = jnp.where(
        row == NEAR_FRONT,
        jnp.where(odd, top, bottom),
        jnp.where(row == FAR_FRONT, jnp.where(odd, bottom, top), 0.0),
    )
    lane = lax.broadcasted_iota(jnp.int32, (count, LANES), 1)
    facing = jnp.where(odd, rim[...], pltpu.roll(rim[...], LANES - rows, 1))
    given = jnp.where(odd, outer[...], pltpu.roll(outer[...], rows, 1))
    given = given * switches[HAS_OUTER : HAS_OUTER + 1, :1]
    sides = jnp.where(lane < rows, facing, jnp.where(lane < 2 * rows, given, 0.0))
    for tile in range(count // TILE):
        message[count + TILE :, tile * LANES : (tile + 1) * LANES] = sides[
            tile * TILE : (tile + 1) * TILE, :
        ]


def first_product(part, below, rim, outer, fronts, switches):
    count, width = part.shape
    return pl.pallas_call(
        first_product_kernel,
        in_specs=[VMEM] * 6,
        out_specs=VMEM,
        out_shape=in_vmem((count + 2 * TILE, width)),
        compiler_params=SMALL,
    )(part, below, rim, outer, fronts, switches)


def second_product_kernel(mine, theirs, fronts, switches, out, given):
    count, width = out.shape
    rows = LANES // 4
    sign = switches[SIGN : SIGN + 1, :1]
    my_ends, their_ends = mine[count : count + 2, :], theirs[count : count + 2, :]
    pieces = []
    for tile in range(count // TILE):
        here, at = pl.ds(tile * TILE, TILE), pl.ds(tile * LANES, LANES)
        my_sides, their_sides = mine[count + TILE :, at], theirs[count + TILE :, at]
        given[here, :] = their_sides
        own = mine[here, :]
        own = own + their_sides[:, rows - 1 : rows] * my_ends[NEAR_FRONT : NEAR_FRONT + 1]
        own = own + their_sides[:, 2 * rows - 1 : 2 * rows] * my_ends[FAR_FRONT : FAR_FRONT + 1]
        other = theirs[here, :]
        other = other + my_sides[:, rows - 1 : rows] * their_ends[NEAR_FRONT : NEAR_FRONT + 1]
        other = other + my_sides[:, 2 * rows - 1 : 2 * rows] * their_ends[FAR_FRONT : FAR_FRONT + 1]
        pieces.append(sign * own + other)
    state = jnp.concatenate(pieces, axis=0)
    out[...] = jnp.dot(state.astype(BF16), fronts[1], preferred_element_type=F32)


def second_product(mine, theirs, fronts, switches):
    count, width = mine.shape[0] - 2 * TILE, mine.shape[1]
    return pl.pallas_call(
        second_product_kernel,
        in_specs=[VMEM] * 4,
        out_specs=[VMEM] * 2,
        out_shape=[in_vmem((count, width)), in_vmem((count, LANES))],
        compiler_params=SMALL,
    )(mine, theirs, fronts, switches)


PIECE = 2


def stencil_kernel(first, field, right, kappa, above, below, given, switches, *rest):
    done, f_in, r_in, k_in, staged, f_sems, r_sems, out_sems, k_sem = rest[-9:]
    block, rows, width = staged.shape
    fields, rights, outs = [], [], []
    for p, at in enumerate(range(0, block, PIECE)):
        here, there = pl.ds(at, PIECE), pl.ds(first + at, PIECE)
        fields.append(pltpu.make_async_copy(field.at[there], f_in.at[here], f_sems.at[p]))
        rights.append(pltpu.make_async_copy(right.at[there], r_in.at[here], r_sems.at[p]))
        outs.append(pltpu.make_async_copy(staged.at[here], done.at[there], out_sems.at[p]))
    kappa_in = pltpu.make_async_copy(kappa, k_in, k_sem)
    kappa_in.start()
    for f_copy, r_copy in zip(fields, rights):
        f_copy.start()
        r_copy.start()
    row = lax.broadcasted_iota(jnp.int32, (rows, width), 0)
    lane = lax.broadcasted_iota(jnp.int32, (rows, width), 1)
    eye_row = lax.broadcasted_iota(jnp.int32, (rows, rows), 0)
    eye = eye_row == lax.broadcasted_iota(jnp.int32, (rows, rows), 1)
    here = pl.ds(first, block)
    odd = switches[ODD : ODD + 1, :1] > 0.0
    top = above[here, :] * switches[HAS_ABOVE : HAS_ABOVE + 1, :1]
    bottom = below[here, :] * switches[HAS_BELOW : HAS_BELOW + 1, :1]
    sides = given[here, :]
    near_side, far_side = sides[:, :rows], sides[:, rows : 2 * rows]
    left, right_col = jnp.where(odd, near_side, far_side), jnp.where(odd, far_side, near_side)
    kappa_in.wait()
    centre = 4.0 + k_in[...]
    for k in range(block):
        if k % PIECE == 0:
            fields[k // PIECE].wait()
            rights[k // PIECE].wait()
        f = f_in[k]
        up = jnp.where(row == 0, top[k : k + 1], pltpu.roll(f, 1, 0))
        down = jnp.where(row == rows - 1, bottom[k : k + 1], pltpu.roll(f, rows - 1, 0))
        west = jnp.sum(jnp.where(eye, left[k : k + 1], 0.0), axis=1, keepdims=True)
        east = jnp.sum(jnp.where(eye, right_col[k : k + 1], 0.0), axis=1, keepdims=True)
        before = jnp.where(lane == 0, west, pltpu.roll(f, 1, 1))
        after = jnp.where(lane == width - 1, east, pltpu.roll(f, width - 1, 1))
        staged[k] = r_in[k] - (centre * f - (down + up + after + before))
        if k % PIECE == PIECE - 1:
            outs[k // PIECE].start()
    for out in outs:
        out.wait()


def stencil(arrays, done, first, block):
    field = arrays[0]
    count, rows, width = field.shape
    specs = [*[HBM] * 3, *[VMEM] * 4]
    arrays = [*[in_hbm(a) for a in arrays[:3]], *arrays[3:]]
    part = block * rows * width
    if done is not None:
        arrays = [*arrays, done]
        specs = [*specs, HBM]
    cube = pltpu.VMEM((block, rows, width), F32)
    return pl.pallas_call(
        functools.partial(stencil_kernel, first),
        in_specs=specs,
        out_specs=HBM,
        out_shape=jax.ShapeDtypeStruct(field.shape, F32),
        scratch_shapes=[
            cube,
            cube,
            pltpu.VMEM((rows, width), F32),
            cube,
            *[pltpu.SemaphoreType.DMA((block // PIECE,))] * 3,
            pltpu.SemaphoreType.DMA(()),
        ],
        input_output_aliases={} if done is None else {7: 0},
        cost_estimate=pl.CostEstimate(flops=8 * part, bytes_accessed=48 * part, transcendentals=0),
        compiler_params=SMALL,
    )(*arrays)


def tied(*values):
    return lax.optimization_barrier(values)


def body(field, right_side, kappa, fronts):
    rows, cols = lax.axis_size("row"), lax.axis_size("col")
    i, j = lax.axis_index("row"), lax.axis_index("col")
    col_bits, row_bits = cols.bit_length() - 1, rows.bit_length() - 1
    odd = j % 2 == 1
    outer_at = jnp.where(odd, j - 2, j + 2)
    has_outer = (outer_at >= 0) & (outer_at < cols)
    values = [odd, i > 0, i < rows - 1, has_outer, jnp.where(odd, -1.0, 1.0)]
    values = jnp.stack([v.astype(F32) for v in values] + [jnp.zeros((), F32)] * (TILE - len(values)))
    switches = jnp.broadcast_to(values[:, None], (TILE, LANES))

    first_row, last_row, part, rim = interface(field, right_side, kappa)
    below = rotated(first_row, "row", -1)
    outer = outer_sides(rim, cols)
    product = first_product(part, below, rim, outer, fronts, switches)

    places = [("col", b, j) for b in range(col_bits)] + [("row", b, i) for b in range(row_bits)]
    top = len(places) - 1

    got = swapped(product, "col", 0)
    product, given = second_product(product, got, fronts, switches)
    above = rotated(last_row, "row", 1)
    arrays = (field, right_side, kappa, above, below, given, switches)
    residual, at = None, 0

    def beside(level, value, residual, at, send):
        share = min(SHARES.get(level, 0), field.shape[0] - at)
        if not share:
            return send(value), residual, at
        value, *rest = tied(value, *arrays[:2], *([] if residual is None else [residual]))
        got = send(value)
        residual = stencil((*rest[:2], *arrays[2:]), rest[2] if rest[2:] else None, at, share)
        got, residual = tied(got, residual)
        return got, residual, at + share

    for level in range(1, top + 1):
        axis, bit, owner = places[level]
        lower = jnp.bitwise_and(jnp.right_shift(owner, bit), 1) == 0
        got, residual, at = beside(level, product, residual, at, lambda v: swapped(v, axis, bit))
        if level < top:
            state = jnp.where(lower, product + got, got - product)
            product = times_front(state, fronts[level + 1])
        else:
            state = times_front_t(got + got, fronts[level])
    for level in range(top - 1, -1, -1):
        axis, bit, owner = places[level]
        lower = jnp.bitwise_and(jnp.right_shift(owner, bit), 1) == 0
        got, residual, at = beside(
            level - top, state, residual, at, lambda v: swapped(v, axis, bit)
        )
        state = times_front_t(jnp.where(lower, state - got, state + got), fronts[level])
    return residual, state


SHARES = {1: 4, 2: 6, 4: 6, -2: 6, -3: 6, -4: 4}


def solution(mesh):
    placed = (P(None, "row", "col"), P(None, "row", "col"), P("row", "col"), P(None, "row", "col"))
    return jax.shard_map(
        body,
        mesh=mesh,
        in_specs=placed,
        out_specs=(P(None, "row", "col"), P("row", "col")),
        check_vma=False,
    )
```

```python
import functools

import jax
import jax.numpy as jnp
from jax import lax
from jax.experimental import pallas as pl
from jax.experimental.pallas import tpu as pltpu
from jax.sharding import PartitionSpec as P

F32 = jnp.float32
BF16 = jnp.bfloat16
TILE = 8
LANES = 128
LOWER, TAKES_LEFT, TAKES_RIGHT, VERTICAL = 0, 1, 2, 3
HAS_ABOVE, HAS_BELOW = 0, 1
WEST_UNIT, EAST_UNIT, PACKED = 0, 1, 2


def switch(switches, tile, row):
    at = tile * TILE + row
    return switches[at : at + 1, :1] > 0.0


def swapped(value, axis, bit):
    count = lax.axis_size(axis)
    return lax.ppermute(value, axis, [(s, s ^ (1 << bit)) for s in range(count)])


def rotated(value, axis, step):
    count = lax.axis_size(axis)
    return lax.ppermute(value, axis, [(s, (s + step) % count) for s in range(count)])


def times_front(value, front):
    return jnp.dot(value.astype(BF16), front, preferred_element_type=F32)


def times_front_t(value, front):
    return lax.dot_general(
        value.astype(BF16), front, (((1,), (1,)), ((), ())), preferred_element_type=F32
    )


def in_vmem(shape):
    return pltpu.VMEM(shape, F32)


def in_hbm(value):
    return pltpu.with_memory_space_constraint(value, pltpu.HBM)


VMEM = pl.BlockSpec(memory_space=pltpu.VMEM)
HBM = pl.BlockSpec(memory_space=pltpu.HBM)
SMALL = pltpu.CompilerParams(vmem_limit_bytes=6 * 2**20)


def interface_kernel(field, right, kappa, first_row, last_row, part, top, bottom, ahead, k8, sems):
    count, rows, width = field.shape
    strip = pl.ds(rows - TILE, TILE)
    copies = [
        pltpu.make_async_copy(field.at[:, pl.ds(0, TILE), :], top, sems.at[0]),
        pltpu.make_async_copy(field.at[:, strip, :], bottom, sems.at[1]),
        pltpu.make_async_copy(kappa.at[strip, :], k8, sems.at[2]),
        pltpu.make_async_copy(right.at[:, strip, :], ahead, sems.at[3]),
    ]
    for copy in copies:
        copy.start()
    lane = lax.broadcasted_iota(jnp.int32, (count, width), 1)
    copies[0].wait()
    first_row[...] = top[:, 0, :]
    copies[1].wait()
    edge = bottom[:, TILE - 1, :]
    last_row[...] = edge
    before = jnp.where(lane == 0, 0.0, pltpu.roll(edge, 1, 1))
    after = jnp.where(lane == width - 1, 0.0, pltpu.roll(edge, width - 1, 1))
    near = bottom[:, TILE - 2, :] + after + before
    copies[2].wait()
    own = (4.0 + k8[TILE - 1 :, :]) * edge - near
    copies[3].wait()
    part[...] = ahead[:, TILE - 1, :] - own


def interface(field, right_side, kappa):
    count, _, width = field.shape
    strip = pltpu.VMEM((count, TILE, width), F32)
    return pl.pallas_call(
        interface_kernel,
        in_specs=[HBM] * 3,
        out_specs=[VMEM] * 3,
        out_shape=[in_vmem((count, width))] * 3,
        scratch_shapes=[
            strip,
            strip,
            strip,
            pltpu.VMEM((TILE, width), F32),
            pltpu.SemaphoreType.DMA((4,)),
        ],
        compiler_params=SMALL,
    )(in_hbm(field), in_hbm(right_side), in_hbm(kappa))


def rims_kernel(field, rim, west, east, sems):
    count, rows, _ = west.shape
    width = field.shape[2]
    half = count // 2
    copies = []
    for p in range(2):
        here = pl.ds(p * half, half)
        first, last = pl.ds(0, LANES), pl.ds(width - LANES, LANES)
        copies.append(pltpu.make_async_copy(field.at[here, :, first], west.at[here], sems.at[2 * p]))
        copies.append(pltpu.make_async_copy(field.at[here, :, last], east.at[here], sems.at[2 * p + 1]))
    for copy in copies:
        copy.start()
    row = lax.broadcasted_iota(jnp.int32, (rows, LANES), 0)
    lane = lax.broadcasted_iota(jnp.int32, (rows, LANES), 1)
    for k in range(count):
        if k % half == 0:
            copies[2 * (k // half)].wait()
            copies[2 * (k // half) + 1].wait()
        first, last = west[k, :, :1], east[k, :, LANES - 1 :]
        spread = jnp.where(lane == row, first, jnp.where(lane == row + rows, last, 0.0))
        rim[k : k + 1, :] = jnp.sum(spread, axis=0, keepdims=True)


def rims(field):
    count, rows, _ = field.shape
    tiles = pltpu.VMEM((count, rows, LANES), F32)
    return pl.pallas_call(
        rims_kernel,
        in_specs=[HBM],
        out_specs=VMEM,
        out_shape=in_vmem((count, LANES)),
        scratch_shapes=[tiles, tiles, pltpu.SemaphoreType.DMA((4,))],
        compiler_params=SMALL,
    )(in_hbm(field))


def packed(rim):
    count = rim.shape[0]
    half = LANES // 2
    pieces = []
    lane = lax.broadcasted_iota(jnp.int32, (count // TILE, LANES), 1)
    for s in range(0, TILE, 2):
        even = rim[pl.ds(s, count // TILE, stride=TILE), :]
        odd = rim[pl.ds(s + 1, count // TILE, stride=TILE), :]
        pieces.append(jnp.where(lane < half, even, pltpu.roll(odd, half, 1)))
    return pieces


def unpack(message, count, rim):
    half = LANES // 2
    at = pl.ds(count + PACKED, count // TILE)
    for s in range(0, TILE, 2):
        piece = message[at, s * half : s * half + LANES]
        rim[pl.ds(s, count // TILE, stride=TILE), :] = piece
        rim[pl.ds(s + 1, count // TILE, stride=TILE), :] = pltpu.roll(piece, half, 1)


def first_product_kernel(part, below, rim, fronts, switches, message):
    count, width = part.shape
    state = part[...] + jnp.where(switch(switches, VERTICAL, HAS_BELOW), below[...], 0.0)
    message[:count, :] = jnp.dot(state.astype(BF16), fronts[0], preferred_element_type=F32)
    top = fronts[0, :16, :].astype(F32)[:1]
    bottom = fronts[0, width - 16 :, :].astype(F32)[15:]
    row = lax.broadcasted_iota(jnp.int32, (TILE, width), 0)
    units = jnp.where(row == WEST_UNIT, top, jnp.where(row == EAST_UNIT, bottom, 0.0))
    message[count : count + TILE, :] = units
    for p, piece in enumerate(packed(rim)):
        at = pl.ds(count + PACKED, count // TILE)
        message[at, p * LANES : (p + 1) * LANES] = piece


def first_product(part, below, rim, fronts, switches):
    count, width = part.shape
    return pl.pallas_call(
        first_product_kernel,
        in_specs=[VMEM] * 5,
        out_specs=VMEM,
        out_shape=in_vmem((count + TILE, width)),
        compiler_params=SMALL,
    )(part, below, rim, fronts, switches)


def next_product_kernel(level, last, mine, theirs, rim, given, fronts, switches, out, *rest):
    next_given, their_rim = rest[-2:]
    count, width = mine.shape[0] - TILE, mine.shape[1]
    rows = LANES // 4
    lower = switch(switches, LOWER, level)
    unpack(theirs, count, their_rim)
    lane = lax.broadcasted_iota(jnp.int32, (count, LANES), 1)
    own, other = rim[...], their_rim[...]
    left = switch(switches, TAKES_LEFT, level) & (lane < rows)
    right = switch(switches, TAKES_RIGHT, level) & (lane >= rows) & (lane < 2 * rows)
    kept = 0.0 if given is None else given[...]
    kept = jnp.where(right, pltpu.roll(other, rows, 1), kept)
    next_given[...] = jnp.where(left, pltpu.roll(other, LANES - rows, 1), kept)

    west, east = count + WEST_UNIT, count + EAST_UNIT
    my_west, my_east = mine[west : west + 1, :], mine[east : east + 1, :]
    their_west, their_east = theirs[west : west + 1, :], theirs[east : east + 1, :]
    into_mine = jnp.where(lower, other[:, rows - 1 : rows], other[:, 2 * rows - 1 : 2 * rows])
    into_theirs = jnp.where(lower, own[:, 2 * rows - 1 : 2 * rows], own[:, rows - 1 : rows])
    my_unit = jnp.where(lower, my_east, my_west)
    their_unit = jnp.where(lower, their_west, their_east)
    total = jnp.where(lower, theirs[:count, :] + mine[:count, :], theirs[:count, :] - mine[:count, :])
    row = lax.broadcasted_iota(jnp.int32, (2 * TILE, width), 0)
    units = jnp.where(row == 0, my_unit, jnp.where(row == 1, their_unit, 0.0))
    if not last:
        west_unit = jnp.where(lower, my_west, their_west)
        east_unit = jnp.where(lower, their_east, -my_east)
        units = jnp.where(row == 2, west_unit, jnp.where(row == 3, east_unit, units))
    rows_in = jnp.concatenate([total.astype(BF16), units.astype(BF16)], axis=0)
    product = jnp.dot(rows_in, fronts[level + 1], preferred_element_type=F32)
    into_mine = jnp.where(lower, into_mine, -into_mine)
    out[:count, :] = (
        product[:count]
        + into_mine * product[count : count + 1]
        + into_theirs * product[count + 1 : count + 2]
    )
    if last:
        return
    out[west : west + 1, :] = product[count + 2 : count + 3]
    out[east : east + 1, :] = product[count + 3 : count + 4]
    at = pl.ds(count + PACKED, count // TILE)
    column = lax.broadcasted_iota(jnp.int32, (count // TILE, width), 1)
    out[at, :] = jnp.where((column % (2 * rows) < rows) == lower, mine[at, :], theirs[at, :])
    spare = count + PACKED + count // TILE
    out[spare:, :] = jnp.zeros((TILE - PACKED - count // TILE, width), F32)
    next_rim = rest[0]
    next_rim[...] = jnp.where((lane < rows) == lower, own, other)


def next_product(level, last, mine, theirs, rim, given, fronts, switches):
    count, width = rim.shape[0], mine.shape[1]
    columns = in_vmem((count, LANES))
    shapes = [in_vmem((count + (0 if last else TILE), width)), *([] if last else [columns]), columns]
    operands = [mine, theirs, rim, *([] if given is None else [given]), fronts, switches]

    def kernel(*refs):
        inputs, others = refs[: len(operands)], refs[len(operands) :]
        if given is None:
            inputs = (*inputs[:3], None, *inputs[3:])
        next_product_kernel(level, last, *inputs, *others)

    out = pl.pallas_call(
        kernel,
        in_specs=[VMEM] * len(operands),
        out_specs=[VMEM] * len(shapes),
        out_shape=shapes,
        scratch_shapes=[pltpu.VMEM((count, LANES), F32)],
        compiler_params=SMALL,
    )(*operands)
    return out if not last else (out[0], None, out[1])


def inner_only_kernel(above, switches, out):
    out[...] = jnp.where(switch(switches, VERTICAL, HAS_ABOVE), above[...], 0.0)


def inner_only(above, switches):
    return pl.pallas_call(
        inner_only_kernel,
        in_specs=[VMEM] * 2,
        out_specs=VMEM,
        out_shape=in_vmem(above.shape),
        cost_estimate=pl.CostEstimate(flops=above.size, bytes_accessed=2**24, transcendentals=0),
        compiler_params=SMALL,
    )(above, switches)


PIECE = 4


def stencil_kernel(first, field, right, kappa, above, below, given, switches, *rest):
    done, f_in, r_in, k_in, staged, f_sems, r_sems, out_sems, k_sem = rest[-9:]
    block, rows, width = staged.shape
    starts = range(0, block, PIECE)
    fields, rights, outs = [], [], []
    for p, at in enumerate(starts):
        size = min(PIECE, block - at)
        here, there = pl.ds(at, size), pl.ds(first + at, size)
        fields.append(pltpu.make_async_copy(field.at[there], f_in.at[here], f_sems.at[p]))
        rights.append(pltpu.make_async_copy(right.at[there], r_in.at[here], r_sems.at[p]))
        outs.append(pltpu.make_async_copy(staged.at[here], done.at[there], out_sems.at[p]))
    kappa_in = pltpu.make_async_copy(kappa, k_in, k_sem)
    kappa_in.start()
    for f_copy, r_copy in zip(fields, rights):
        f_copy.start()
        r_copy.start()
    row = lax.broadcasted_iota(jnp.int32, (rows, width), 0)
    lane = lax.broadcasted_iota(jnp.int32, (rows, width), 1)
    cells = jnp.transpose(given[...])
    has_below = switch(switches, VERTICAL, HAS_BELOW)
    kappa_in.wait()
    centre = 4.0 + k_in[...]
    for p, at in enumerate(starts):
        fields[p].wait()
        rights[p].wait()
        for k in range(at, min(at + PIECE, block)):
            line = slice(first + k, first + k + 1)
            f = f_in[k]
            bottom = jnp.where(has_below, below[line, :], 0.0)
            up = jnp.where(row == 0, above[line, :], pltpu.roll(f, 1, 0))
            down = jnp.where(row == rows - 1, bottom, pltpu.roll(f, rows - 1, 0))
            west, east = cells[:rows, line], cells[rows : 2 * rows, line]
            before = jnp.where(lane == 0, west, pltpu.roll(f, 1, 1))
            after = jnp.where(lane == width - 1, east, pltpu.roll(f, width - 1, 1))
            staged[k] = r_in[k] - (centre * f - (down + up + after + before))
        outs[p].start()
    for out in outs:
        out.wait()


def stencil(arrays, done, first, block):
    field = arrays[0]
    count, rows, width = field.shape
    specs = [*[HBM] * 3, *[VMEM] * 4]
    arrays = [*[in_hbm(a) for a in arrays[:3]], *arrays[3:]]
    part = block * rows * width
    if done is not None:
        arrays = [*arrays, done]
        specs = [*specs, HBM]
    cube = pltpu.VMEM((block, rows, width), F32)
    return pl.pallas_call(
        functools.partial(stencil_kernel, first),
        in_specs=specs,
        out_specs=HBM,
        out_shape=jax.ShapeDtypeStruct(field.shape, F32),
        scratch_shapes=[
            cube,
            cube,
            pltpu.VMEM((rows, width), F32),
            cube,
            *[pltpu.SemaphoreType.DMA((-(-block // PIECE),))] * 3,
            pltpu.SemaphoreType.DMA(()),
        ],
        input_output_aliases={} if done is None else {7: 0},
        cost_estimate=pl.CostEstimate(flops=8 * part, bytes_accessed=48 * part, transcendentals=0),
        compiler_params=SMALL,
    )(*arrays)


def tied(*values):
    return lax.optimization_barrier(values)


def all_switches(i, j, rows):
    level = lax.broadcasted_iota(jnp.int32, (TILE, LANES), 0)
    upper = jnp.bitwise_and(jnp.right_shift(j, level), 1) == 1
    ones = jnp.left_shift(1, level) - 1
    within = jnp.bitwise_and(j, ones)
    vertical = jnp.where(level == HAS_ABOVE, i > 0, i < rows - 1)
    tiles = [~upper, upper & (within == 0), ~upper & (within == ones), vertical]
    return jnp.concatenate(tiles, axis=0).astype(F32)


def body(field, right_side, kappa, fronts):
    rows, cols = lax.axis_size("row"), lax.axis_size("col")
    i, j = lax.axis_index("row"), lax.axis_index("col")
    col_bits, row_bits = cols.bit_length() - 1, rows.bit_length() - 1
    switches = all_switches(i, j, rows)
    places = [("col", b, j) for b in range(col_bits)] + [("row", b, i) for b in range(row_bits)]
    top = len(places) - 1

    first_row, last_row, part = interface(field, right_side, kappa)
    below = rotated(first_row, "row", -1)
    above = rotated(last_row, "row", 1)
    first_row, rim_field = tied(first_row, field)
    rim = rims(rim_field)
    product = first_product(part, below, rim, fronts, switches)
    given = None
    for level in range(col_bits):
        if level == 1:
            product, above = tied(product, above)
        got = swapped(product, "col", level)
        if level == 1:
            above = inner_only(above, switches)
            got, above = tied(got, above)
        last = level == col_bits - 1
        product, rim, given = next_product(level, last, product, got, rim, given, fronts, switches)
    arrays = (field, right_side, kappa, above, below, given, switches)
    residual, at = None, 0

    def beside(step, value, residual, at, send):
        left = field.shape[0] - at
        share = left if step == -top else min(SHARES.get(step, 0), left)
        if not share:
            return send(value), residual, at
        value, *rest = tied(value, *arrays[:2], *([] if residual is None else [residual]))
        got = send(value)
        residual = stencil((*rest[:2], *arrays[2:]), rest[2] if rest[2:] else None, at, share)
        got, residual = tied(got, residual)
        return got, residual, at + share

    for level in range(col_bits, top + 1):
        axis, bit, owner = places[level]
        lower = jnp.bitwise_and(jnp.right_shift(owner, bit), 1) == 0
        got, residual, at = beside(
            level - top, product, residual, at, lambda v: swapped(v, axis, bit)
        )
        if level < top:
            state = jnp.where(lower, product + got, got - product)
            product = times_front(state, fronts[level + 1])
        else:
            state = times_front_t(got + got, fronts[level])
    for level in range(top - 1, -1, -1):
        axis, bit, owner = places[level]
        lower = jnp.bitwise_and(jnp.right_shift(owner, bit), 1) == 0
        got, residual, at = beside(
            level - top, state, residual, at, lambda v: swapped(v, axis, bit)
        )
        state = times_front_t(jnp.where(lower, state - got, state + got), fronts[level])
    return residual, state


SHARES = {0: 6, -2: 12, -3: 7}


def solution(mesh):
    placed = (P(None, "row", "col"), P(None, "row", "col"), P("row", "col"), P(None, "row", "col"))
    return jax.shard_map(
        body,
        mesh=mesh,
        in_specs=placed,
        out_specs=(P(None, "row", "col"), P("row", "col")),
        check_vma=False,
    )
```

```python
import functools

import jax
import jax.numpy as jnp
from jax import lax
from jax.experimental import pallas as pl
from jax.experimental.pallas import tpu as pltpu
from jax.sharding import PartitionSpec as P

F32 = jnp.float32
BF16 = jnp.bfloat16
TILE = 8
LANES = 128
WEST_UNIT, EAST_UNIT, PACKED = 0, 1, 2


def is_lower(level):
    return jnp.bitwise_and(jnp.right_shift(lax.axis_index("col"), level), 1) == 0


def swapped(value, axis, bit):
    count = lax.axis_size(axis)
    return lax.ppermute(value, axis, [(s, s ^ (1 << bit)) for s in range(count)])


def rotated(value, axis, step):
    count = lax.axis_size(axis)
    return lax.ppermute(value, axis, [(s, (s + step) % count) for s in range(count)])


def times_front(value, front):
    return jnp.dot(value.astype(BF16), front, preferred_element_type=F32)


def times_front_t(value, front):
    return lax.dot_general(
        value.astype(BF16), front, (((1,), (1,)), ((), ())), preferred_element_type=F32
    )


def in_vmem(shape):
    return pltpu.VMEM(shape, F32)


def in_hbm(value):
    return pltpu.with_memory_space_constraint(value, pltpu.HBM)


VMEM = pl.BlockSpec(memory_space=pltpu.VMEM)
HBM = pl.BlockSpec(memory_space=pltpu.HBM)
SMALL = pltpu.CompilerParams(vmem_limit_bytes=6 * 2**20)


def interface_kernel(field, right, kappa, first_row, last_row, part, inner, ahead, k1, sems):
    count, rows, width = field.shape
    end = rows - 1
    copies = [
        pltpu.make_async_copy(field.at[:, 0, :], first_row, sems.at[0]),
        pltpu.make_async_copy(field.at[:, end, :], last_row, sems.at[1]),
        pltpu.make_async_copy(field.at[:, end - 1, :], inner, sems.at[2]),
        pltpu.make_async_copy(right.at[:, end, :], ahead, sems.at[3]),
        pltpu.make_async_copy(kappa.at[pl.ds(end, 1), :], k1, sems.at[4]),
    ]
    for copy in copies:
        copy.start()
    lane = lax.broadcasted_iota(jnp.int32, (count, width), 1)
    for copy in copies[1:]:
        copy.wait()
    edge = last_row[...]
    before = jnp.where(lane == 0, 0.0, pltpu.roll(edge, 1, 1))
    after = jnp.where(lane == width - 1, 0.0, pltpu.roll(edge, width - 1, 1))
    part[...] = ahead[...] - ((4.0 + k1[...]) * edge - (inner[...] + after + before))
    copies[0].wait()


def interface(field, right_side, kappa):
    count, _, width = field.shape
    line = pltpu.VMEM((count, width), F32)
    return pl.pallas_call(
        interface_kernel,
        in_specs=[HBM] * 3,
        out_specs=[VMEM] * 3,
        out_shape=[in_vmem((count, width))] * 3,
        scratch_shapes=[line, line, pltpu.VMEM((1, width), F32), pltpu.SemaphoreType.DMA((5,))],
        compiler_params=SMALL,
    )(in_hbm(field), in_hbm(right_side), in_hbm(kappa))


def rims_kernel(field, rim, west, east, sems):
    count, rows, _ = west.shape
    width = field.shape[2]
    half = count // 2
    copies = []
    for p in range(2):
        here = pl.ds(p * half, half)
        first, last = pl.ds(0, LANES), pl.ds(width - LANES, LANES)
        copies.append(pltpu.make_async_copy(field.at[here, :, first], west.at[here], sems.at[2 * p]))
        copies.append(pltpu.make_async_copy(field.at[here, :, last], east.at[here], sems.at[2 * p + 1]))
    for copy in copies:
        copy.start()
    row = lax.broadcasted_iota(jnp.int32, (rows, LANES), 0)
    lane = lax.broadcasted_iota(jnp.int32, (rows, LANES), 1)
    for k in range(count):
        if k % half == 0:
            copies[2 * (k // half)].wait()
            copies[2 * (k // half) + 1].wait()
        first, last = west[k, :, :1], east[k, :, LANES - 1 :]
        spread = jnp.where(lane == row, first, jnp.where(lane == row + rows, last, 0.0))
        rim[k : k + 1, :] = jnp.sum(spread, axis=0, keepdims=True)


def rims(field):
    count, rows, _ = field.shape
    tiles = pltpu.VMEM((count, rows, LANES), F32)
    return pl.pallas_call(
        rims_kernel,
        in_specs=[HBM],
        out_specs=VMEM,
        out_shape=in_vmem((count, LANES)),
        scratch_shapes=[tiles, tiles, pltpu.SemaphoreType.DMA((4,))],
        compiler_params=SMALL,
    )(in_hbm(field))


def packed(rim):
    count = rim.shape[0]
    half = LANES // 2
    pieces = []
    lane = lax.broadcasted_iota(jnp.int32, (count // TILE, LANES), 1)
    for s in range(0, TILE, 2):
        even = rim[pl.ds(s, count // TILE, stride=TILE), :]
        odd = rim[pl.ds(s + 1, count // TILE, stride=TILE), :]
        pieces.append(jnp.where(lane < half, even, pltpu.roll(odd, half, 1)))
    return pieces


def unpack(message, count, rim):
    half = LANES // 2
    at = pl.ds(count + PACKED, count // TILE)
    for s in range(0, TILE, 2):
        piece = message[at, s * half : s * half + LANES]
        rim[pl.ds(s, count // TILE, stride=TILE), :] = piece
        rim[pl.ds(s + 1, count // TILE, stride=TILE), :] = pltpu.roll(piece, half, 1)


def first_product_kernel(has_rows, part, below, rim, fronts, message):
    count, width = part.shape
    has_below = lax.axis_index("row") < has_rows - 1
    state = part[...] + jnp.where(has_below, below[...], 0.0)
    message[:count, :] = jnp.dot(state.astype(BF16), fronts[0], preferred_element_type=F32)
    top = fronts[0, :16, :].astype(F32)[:1]
    bottom = fronts[0, width - 16 :, :].astype(F32)[15:]
    row = lax.broadcasted_iota(jnp.int32, (TILE, width), 0)
    units = jnp.where(row == WEST_UNIT, top, jnp.where(row == EAST_UNIT, bottom, 0.0))
    message[count : count + TILE, :] = units
    for p, piece in enumerate(packed(rim)):
        at = pl.ds(count + PACKED, count // TILE)
        message[at, p * LANES : (p + 1) * LANES] = piece


def first_product(part, below, rim, fronts):
    count, width = part.shape
    return pl.pallas_call(
        functools.partial(first_product_kernel, lax.axis_size("row")),
        in_specs=[VMEM] * 4,
        out_specs=VMEM,
        out_shape=in_vmem((count + TILE, width)),
        compiler_params=SMALL,
    )(part, below, rim, fronts)


def next_product_kernel(level, last, mine, theirs, rim, given, fronts, out, *rest):
    next_given, their_rim = rest[-2:]
    count, width = mine.shape[0] - TILE, mine.shape[1]
    rows = LANES // 4
    lower = is_lower(level)
    ones = 2**level - 1
    within = jnp.bitwise_and(lax.axis_index("col"), ones)
    unpack(theirs, count, their_rim)
    lane = lax.broadcasted_iota(jnp.int32, (count, LANES), 1)
    own, other = rim[...], their_rim[...]
    takes_left = jnp.logical_and(jnp.logical_not(lower), within == 0)
    takes_right = jnp.logical_and(lower, within == ones)
    left, right = lane < rows, jnp.bitwise_and(lane, 3 * rows) == rows
    kept = jnp.zeros(other.shape, F32) if given is None else given[...]
    from_right = jnp.where(right, pltpu.roll(other, rows, 1), kept)
    kept = jnp.where(takes_right, from_right, kept)
    from_left = jnp.where(left, pltpu.roll(other, LANES - rows, 1), kept)
    next_given[...] = jnp.where(takes_left, from_left, kept)

    west, east = count + WEST_UNIT, count + EAST_UNIT
    my_west, my_east = mine[west : west + 1, :], mine[east : east + 1, :]
    their_west, their_east = theirs[west : west + 1, :], theirs[east : east + 1, :]
    into_mine = jnp.where(lower, other[:, rows - 1 : rows], other[:, 2 * rows - 1 : 2 * rows])
    into_theirs = jnp.where(lower, own[:, 2 * rows - 1 : 2 * rows], own[:, rows - 1 : rows])
    my_unit = jnp.where(lower, my_east, my_west)
    their_unit = jnp.where(lower, their_west, their_east)
    total = jnp.where(lower, theirs[:count, :] + mine[:count, :], theirs[:count, :] - mine[:count, :])
    row = lax.broadcasted_iota(jnp.int32, (2 * TILE, width), 0)
    units = jnp.where(row == 0, my_unit, jnp.where(row == 1, their_unit, 0.0))
    if not last:
        west_unit = jnp.where(lower, my_west, their_west)
        east_unit = jnp.where(lower, their_east, -my_east)
        units = jnp.where(row == 2, west_unit, jnp.where(row == 3, east_unit, units))
    rows_in = jnp.concatenate([total.astype(BF16), units.astype(BF16)], axis=0)
    product = jnp.dot(rows_in, fronts[level + 1], preferred_element_type=F32)
    into_mine = jnp.where(lower, into_mine, -into_mine)
    out[:count, :] = (
        product[:count]
        + into_mine * product[count : count + 1]
        + into_theirs * product[count + 1 : count + 2]
    )
    if last:
        return
    out[west : west + 1, :] = product[count + 2 : count + 3]
    out[east : east + 1, :] = product[count + 3 : count + 4]
    at = pl.ds(count + PACKED, count // TILE)
    turn = jnp.where(lower, 0, rows)
    column = lax.broadcasted_iota(jnp.int32, (count // TILE, width), 1)
    keeps = jnp.bitwise_and(column + turn, rows) == 0
    out[at, :] = jnp.where(keeps, mine[at, :], theirs[at, :])
    spare = count + PACKED + count // TILE
    out[spare:, :] = jnp.zeros((TILE - PACKED - count // TILE, width), F32)
    next_rim = rest[0]
    next_rim[...] = jnp.where(jnp.bitwise_and(lane + turn, rows) == 0, own, other)


def next_product(level, last, mine, theirs, rim, given, fronts):
    count, width = rim.shape[0], mine.shape[1]
    columns = in_vmem((count, LANES))
    shapes = [in_vmem((count + (0 if last else TILE), width)), *([] if last else [columns]), columns]
    operands = [mine, theirs, rim, *([] if given is None else [given]), fronts]

    def kernel(*refs):
        inputs, others = refs[: len(operands)], refs[len(operands) :]
        if given is None:
            inputs = (*inputs[:3], None, *inputs[3:])
        next_product_kernel(level, last, *inputs, *others)

    out = pl.pallas_call(
        kernel,
        in_specs=[VMEM] * len(operands),
        out_specs=[VMEM] * len(shapes),
        out_shape=shapes,
        scratch_shapes=[pltpu.VMEM((count, LANES), F32)],
        compiler_params=SMALL,
    )(*operands)
    return out if not last else (out[0], None, out[1])


def inner_only_kernel(above, out):
    out[...] = jnp.where(lax.axis_index("row") > 0, above[...], 0.0)


def inner_only(above):
    return pl.pallas_call(
        inner_only_kernel,
        in_specs=[VMEM],
        out_specs=VMEM,
        out_shape=in_vmem(above.shape),
        cost_estimate=pl.CostEstimate(flops=above.size, bytes_accessed=2**24, transcendentals=0),
        compiler_params=SMALL,
    )(above)


PIECE = 4


def stencil_kernel(has_rows, first, field, right, kappa, above, below, given, *rest):
    done, f_in, r_in, k_in, staged, f_sems, r_sems, out_sems, k_sem = rest[-9:]
    block, rows, width = staged.shape
    starts = range(0, block, PIECE)
    fields, rights, outs = [], [], []
    for p, at in enumerate(starts):
        size = min(PIECE, block - at)
        here, there = pl.ds(at, size), pl.ds(first + at, size)
        fields.append(pltpu.make_async_copy(field.at[there], f_in.at[here], f_sems.at[p]))
        rights.append(pltpu.make_async_copy(right.at[there], r_in.at[here], r_sems.at[p]))
        outs.append(pltpu.make_async_copy(staged.at[here], done.at[there], out_sems.at[p]))
    kappa_in = pltpu.make_async_copy(kappa, k_in, k_sem)
    kappa_in.start()
    for f_copy, r_copy in zip(fields, rights):
        f_copy.start()
        r_copy.start()
    row = lax.broadcasted_iota(jnp.int32, (rows, width), 0)
    lane = lax.broadcasted_iota(jnp.int32, (rows, width), 1)
    cells = jnp.transpose(given[...])
    has_below = lax.axis_index("row") < has_rows - 1
    kappa_in.wait()
    centre = 4.0 + k_in[...]
    for p, at in enumerate(starts):
        fields[p].wait()
        rights[p].wait()
        for k in range(at, min(at + PIECE, block)):
            line = slice(first + k, first + k + 1)
            f = f_in[k]
            bottom = jnp.where(has_below, below[line, :], 0.0)
            up = jnp.where(row == 0, above[line, :], pltpu.roll(f, 1, 0))
            down = jnp.where(row == rows - 1, bottom, pltpu.roll(f, rows - 1, 0))
            west, east = cells[:rows, line], cells[rows : 2 * rows, line]
            before = jnp.where(lane == 0, west, pltpu.roll(f, 1, 1))
            after = jnp.where(lane == width - 1, east, pltpu.roll(f, width - 1, 1))
            staged[k] = r_in[k] - (centre * f - (down + up + after + before))
        outs[p].start()
    for out in outs:
        out.wait()


def stencil(arrays, done, first, block):
    field = arrays[0]
    count, rows, width = field.shape
    specs = [*[HBM] * 3, *[VMEM] * 3]
    arrays = [*[in_hbm(a) for a in arrays[:3]], *arrays[3:]]
    part = block * rows * width
    if done is not None:
        arrays = [*arrays, done]
        specs = [*specs, HBM]
    cube = pltpu.VMEM((block, rows, width), F32)
    return pl.pallas_call(
        functools.partial(stencil_kernel, lax.axis_size("row"), first),
        in_specs=specs,
        out_specs=HBM,
        out_shape=jax.ShapeDtypeStruct(field.shape, F32),
        scratch_shapes=[
            cube,
            cube,
            pltpu.VMEM((rows, width), F32),
            cube,
            *[pltpu.SemaphoreType.DMA((-(-block // PIECE),))] * 3,
            pltpu.SemaphoreType.DMA(()),
        ],
        input_output_aliases={} if done is None else {6: 0},
        cost_estimate=pl.CostEstimate(flops=8 * part, bytes_accessed=48 * part, transcendentals=0),
        compiler_params=SMALL,
    )(*arrays)


def tied(*values):
    return lax.optimization_barrier(values)


def body(field, right_side, kappa, fronts):
    rows, cols = lax.axis_size("row"), lax.axis_size("col")
    i, j = lax.axis_index("row"), lax.axis_index("col")
    col_bits, row_bits = cols.bit_length() - 1, rows.bit_length() - 1
    places = [("col", b, j) for b in range(col_bits)] + [("row", b, i) for b in range(row_bits)]
    top = len(places) - 1

    first_row, last_row, part = interface(field, right_side, kappa)
    below = rotated(first_row, "row", -1)
    above = rotated(last_row, "row", 1)
    first_row, rim_field = tied(first_row, field)
    rim = rims(rim_field)
    product = first_product(part, below, rim, fronts)
    given = None
    for level in range(col_bits):
        if level == 1:
            product, above = tied(product, above)
        got = swapped(product, "col", level)
        if level == 1:
            above = inner_only(above)
            got, above = tied(got, above)
        last = level == col_bits - 1
        product, rim, given = next_product(level, last, product, got, rim, given, fronts)
    arrays = (field, right_side, kappa, above, below, given)
    residual, at = None, 0

    def beside(step, value, residual, at, send):
        left = field.shape[0] - at
        share = left if step == -top else min(SHARES.get(step, 0), left)
        if not share:
            return send(value), residual, at
        value, *rest = tied(value, *arrays[:2], *([] if residual is None else [residual]))
        got = send(value)
        residual = stencil((*rest[:2], *arrays[2:]), rest[2] if rest[2:] else None, at, share)
        got, residual = tied(got, residual)
        return got, residual, at + share

    for level in range(col_bits, top + 1):
        axis, bit, owner = places[level]
        lower = jnp.bitwise_and(jnp.right_shift(owner, bit), 1) == 0
        got, residual, at = beside(
            level - top, product, residual, at, lambda v: swapped(v, axis, bit)
        )
        if level < top:
            state = jnp.where(lower, product + got, got - product)
            product = times_front(state, fronts[level + 1])
        else:
            state = times_front_t(got + got, fronts[level])
    for level in range(top - 1, -1, -1):
        axis, bit, owner = places[level]
        lower = jnp.bitwise_and(jnp.right_shift(owner, bit), 1) == 0
        got, residual, at = beside(
            level - top, state, residual, at, lambda v: swapped(v, axis, bit)
        )
        state = times_front_t(jnp.where(lower, state - got, state + got), fronts[level])
    return residual, state


SHARES = {0: 6, -2: 12, -3: 7}


def solution(mesh):
    placed = (P(None, "row", "col"), P(None, "row", "col"), P("row", "col"), P(None, "row", "col"))
    return jax.shard_map(
        body,
        mesh=mesh,
        in_specs=placed,
        out_specs=(P(None, "row", "col"), P("row", "col")),
        check_vma=False,
    )
```

```python
import functools

import jax
import jax.numpy as jnp
from jax import lax
from jax.experimental import pallas as pl
from jax.experimental.pallas import tpu as pltpu
from jax.sharding import PartitionSpec as P

F32 = jnp.float32
BF16 = jnp.bfloat16
TILE = 8
LANES = 128
WEST_UNIT, EAST_UNIT, PACKED = 0, 1, 2


def is_lower(level):
    return jnp.bitwise_and(jnp.right_shift(lax.axis_index("col"), level), 1) == 0


def swapped(value, axis, bit):
    count = lax.axis_size(axis)
    return lax.ppermute(value, axis, [(s, s ^ (1 << bit)) for s in range(count)])


def rotated(value, axis, step):
    count = lax.axis_size(axis)
    return lax.ppermute(value, axis, [(s, (s + step) % count) for s in range(count)])


def times_front(value, front):
    return jnp.dot(value.astype(BF16), front, preferred_element_type=F32)


def times_front_t(value, front):
    return lax.dot_general(
        value.astype(BF16), front, (((1,), (1,)), ((), ())), preferred_element_type=F32
    )


def in_vmem(shape):
    return pltpu.VMEM(shape, F32)


def in_hbm(value):
    return pltpu.with_memory_space_constraint(value, pltpu.HBM)


VMEM = pl.BlockSpec(memory_space=pltpu.VMEM)
HBM = pl.BlockSpec(memory_space=pltpu.HBM)
SMALL = pltpu.CompilerParams(vmem_limit_bytes=6 * 2**20)


def first_row_kernel(field, out, sem):
    copy = pltpu.make_async_copy(field.at[:, 0, :], out, sem)
    copy.start()
    copy.wait()


def first_row_of(field):
    count, _, width = field.shape
    return pl.pallas_call(
        first_row_kernel,
        in_specs=[HBM],
        out_specs=VMEM,
        out_shape=in_vmem((count, width)),
        scratch_shapes=[pltpu.SemaphoreType.DMA(())],
        compiler_params=SMALL,
    )(in_hbm(field))


def interface_kernel(field, right, kappa, last_row, part, rim, ahead, k1, sems):
    count, rows, width = field.shape
    end = rows - 1
    copies = [
        pltpu.make_async_copy(kappa.at[pl.ds(end, 1), :], k1, sems.at[0]),
        pltpu.make_async_copy(right.at[:, end, :], ahead, sems.at[1]),
    ]
    for copy in copies:
        copy.start()
    row = lax.broadcasted_iota(jnp.int32, (rows, LANES), 0)
    lane = lax.broadcasted_iota(jnp.int32, (rows, LANES), 1)
    for k in range(count):
        first, last = field[k, :, :1], field[k, :, width - 1 :]
        spread = jnp.where(lane == row, first, jnp.where(lane == row + rows, last, 0.0))
        rim[k : k + 1, :] = jnp.sum(spread, axis=0, keepdims=True)
    lane = lax.broadcasted_iota(jnp.int32, (count, width), 1)
    edge = field[:, end, :]
    last_row[...] = edge
    before = jnp.where(lane == 0, 0.0, pltpu.roll(edge, 1, 1))
    after = jnp.where(lane == width - 1, 0.0, pltpu.roll(edge, width - 1, 1))
    near = field[:, end - 1, :] + after + before
    for copy in copies:
        copy.wait()
    part[...] = ahead[...] - ((4.0 + k1[...]) * edge - near)


def interface(field, right_side, kappa):
    count, _, width = field.shape
    return pl.pallas_call(
        interface_kernel,
        in_specs=[VMEM, HBM, HBM],
        out_specs=[VMEM] * 3,
        out_shape=[in_vmem((count, width))] * 2 + [in_vmem((count, LANES))],
        scratch_shapes=[
            pltpu.VMEM((count, width), F32),
            pltpu.VMEM((1, width), F32),
            pltpu.SemaphoreType.DMA((2,)),
        ],
        compiler_params=SMALL,
    )(pltpu.with_memory_space_constraint(field, pltpu.VMEM), in_hbm(right_side), in_hbm(kappa))


def packed(rim):
    count = rim.shape[0]
    half = LANES // 2
    pieces = []
    lane = lax.broadcasted_iota(jnp.int32, (count // TILE, LANES), 1)
    for s in range(0, TILE, 2):
        even = rim[pl.ds(s, count // TILE, stride=TILE), :]
        odd = rim[pl.ds(s + 1, count // TILE, stride=TILE), :]
        pieces.append(jnp.where(lane < half, even, pltpu.roll(odd, half, 1)))
    return pieces


def unpack(message, count, rim):
    half = LANES // 2
    at = pl.ds(count + PACKED, count // TILE)
    for s in range(0, TILE, 2):
        piece = message[at, s * half : s * half + LANES]
        rim[pl.ds(s, count // TILE, stride=TILE), :] = piece
        rim[pl.ds(s + 1, count // TILE, stride=TILE), :] = pltpu.roll(piece, half, 1)


def first_product_kernel(has_rows, part, below, rim, fronts, message):
    count, width = part.shape
    has_below = lax.axis_index("row") < has_rows - 1
    state = part[...] + jnp.where(has_below, below[...], 0.0)
    message[:count, :] = jnp.dot(state.astype(BF16), fronts[0], preferred_element_type=F32)
    top = fronts[0, :16, :].astype(F32)[:1]
    bottom = fronts[0, width - 16 :, :].astype(F32)[15:]
    row = lax.broadcasted_iota(jnp.int32, (TILE, width), 0)
    units = jnp.where(row == WEST_UNIT, top, jnp.where(row == EAST_UNIT, bottom, 0.0))
    message[count : count + TILE, :] = units
    for p, piece in enumerate(packed(rim)):
        at = pl.ds(count + PACKED, count // TILE)
        message[at, p * LANES : (p + 1) * LANES] = piece


def first_product(part, below, rim, fronts):
    count, width = part.shape
    return pl.pallas_call(
        functools.partial(first_product_kernel, lax.axis_size("row")),
        in_specs=[VMEM] * 4,
        out_specs=VMEM,
        out_shape=in_vmem((count + TILE, width)),
        compiler_params=SMALL,
    )(part, below, rim, fronts)


def next_product_kernel(level, last, mine, theirs, rim, given, fronts, out, *rest):
    next_given, their_rim = rest[-2:]
    count, width = mine.shape[0] - TILE, mine.shape[1]
    rows = LANES // 4
    lower = is_lower(level)
    ones = 2**level - 1
    within = jnp.bitwise_and(lax.axis_index("col"), ones)
    unpack(theirs, count, their_rim)
    lane = lax.broadcasted_iota(jnp.int32, (count, LANES), 1)
    own, other = rim[...], their_rim[...]
    takes_left = jnp.logical_and(jnp.logical_not(lower), within == 0)
    takes_right = jnp.logical_and(lower, within == ones)
    left, right = lane < rows, jnp.bitwise_and(lane, 3 * rows) == rows
    kept = jnp.zeros(other.shape, F32) if given is None else given[...]
    from_right = jnp.where(right, pltpu.roll(other, rows, 1), kept)
    kept = jnp.where(takes_right, from_right, kept)
    from_left = jnp.where(left, pltpu.roll(other, LANES - rows, 1), kept)
    next_given[...] = jnp.where(takes_left, from_left, kept)

    west, east = count + WEST_UNIT, count + EAST_UNIT
    my_west, my_east = mine[west : west + 1, :], mine[east : east + 1, :]
    their_west, their_east = theirs[west : west + 1, :], theirs[east : east + 1, :]
    into_mine = jnp.where(lower, other[:, rows - 1 : rows], other[:, 2 * rows - 1 : 2 * rows])
    into_theirs = jnp.where(lower, own[:, 2 * rows - 1 : 2 * rows], own[:, rows - 1 : rows])
    my_unit = jnp.where(lower, my_east, my_west)
    their_unit = jnp.where(lower, their_west, their_east)
    total = jnp.where(lower, theirs[:count, :] + mine[:count, :], theirs[:count, :] - mine[:count, :])
    row = lax.broadcasted_iota(jnp.int32, (2 * TILE, width), 0)
    units = jnp.where(row == 0, my_unit, jnp.where(row == 1, their_unit, 0.0))
    if not last:
        west_unit = jnp.where(lower, my_west, their_west)
        east_unit = jnp.where(lower, their_east, -my_east)
        units = jnp.where(row == 2, west_unit, jnp.where(row == 3, east_unit, units))
    rows_in = jnp.concatenate([total.astype(BF16), units.astype(BF16)], axis=0)
    product = jnp.dot(rows_in, fronts[level + 1], preferred_element_type=F32)
    into_mine = jnp.where(lower, into_mine, -into_mine)
    out[:count, :] = (
        product[:count]
        + into_mine * product[count : count + 1]
        + into_theirs * product[count + 1 : count + 2]
    )
    if last:
        return
    out[west : west + 1, :] = product[count + 2 : count + 3]
    out[east : east + 1, :] = product[count + 3 : count + 4]
    at = pl.ds(count + PACKED, count // TILE)
    turn = jnp.where(lower, 0, rows)
    column = lax.broadcasted_iota(jnp.int32, (count // TILE, width), 1)
    keeps = jnp.bitwise_and(column + turn, rows) == 0
    out[at, :] = jnp.where(keeps, mine[at, :], theirs[at, :])
    spare = count + PACKED + count // TILE
    out[spare:, :] = jnp.zeros((TILE - PACKED - count // TILE, width), F32)
    next_rim = rest[0]
    next_rim[...] = jnp.where(jnp.bitwise_and(lane + turn, rows) == 0, own, other)


def next_product(level, last, mine, theirs, rim, given, fronts):
    count, width = rim.shape[0], mine.shape[1]
    columns = in_vmem((count, LANES))
    shapes = [in_vmem((count + (0 if last else TILE), width)), *([] if last else [columns]), columns]
    operands = [mine, theirs, rim, *([] if given is None else [given]), fronts]

    def kernel(*refs):
        inputs, others = refs[: len(operands)], refs[len(operands) :]
        if given is None:
            inputs = (*inputs[:3], None, *inputs[3:])
        next_product_kernel(level, last, *inputs, *others)

    out = pl.pallas_call(
        kernel,
        in_specs=[VMEM] * len(operands),
        out_specs=[VMEM] * len(shapes),
        out_shape=shapes,
        scratch_shapes=[pltpu.VMEM((count, LANES), F32)],
        compiler_params=SMALL,
    )(*operands)
    return out if not last else (out[0], None, out[1])


def inner_only_kernel(above, out):
    out[...] = jnp.where(lax.axis_index("row") > 0, above[...], 0.0)


def inner_only(above):
    return pl.pallas_call(
        inner_only_kernel,
        in_specs=[VMEM],
        out_specs=VMEM,
        out_shape=in_vmem(above.shape),
        cost_estimate=pl.CostEstimate(flops=above.size, bytes_accessed=2**24, transcendentals=0),
        compiler_params=SMALL,
    )(above)


PIECE = 4


def stencil_kernel(has_rows, first, field, right, kappa, above, below, given, *rest):
    done, f_in, r_in, k_in, staged, f_sems, r_sems, out_sems, k_sem = rest[-9:]
    block, rows, width = staged.shape
    starts = range(0, block, PIECE)
    fields, rights, outs = [], [], []
    for p, at in enumerate(starts):
        size = min(PIECE, block - at)
        here, there = pl.ds(at, size), pl.ds(first + at, size)
        fields.append(pltpu.make_async_copy(field.at[there], f_in.at[here], f_sems.at[p]))
        rights.append(pltpu.make_async_copy(right.at[there], r_in.at[here], r_sems.at[p]))
        outs.append(pltpu.make_async_copy(staged.at[here], done.at[there], out_sems.at[p]))
    kappa_in = pltpu.make_async_copy(kappa, k_in, k_sem)
    kappa_in.start()
    for f_copy, r_copy in zip(fields, rights):
        f_copy.start()
        r_copy.start()
    row = lax.broadcasted_iota(jnp.int32, (rows, width), 0)
    lane = lax.broadcasted_iota(jnp.int32, (rows, width), 1)
    cells = jnp.transpose(given[...])
    has_below = lax.axis_index("row") < has_rows - 1
    kappa_in.wait()
    centre = 4.0 + k_in[...]
    for p, at in enumerate(starts):
        fields[p].wait()
        rights[p].wait()
        for k in range(at, min(at + PIECE, block)):
            line = slice(first + k, first + k + 1)
            f = f_in[k]
            bottom = jnp.where(has_below, below[line, :], 0.0)
            up = jnp.where(row == 0, above[line, :], pltpu.roll(f, 1, 0))
            down = jnp.where(row == rows - 1, bottom, pltpu.roll(f, rows - 1, 0))
            west, east = cells[:rows, line], cells[rows : 2 * rows, line]
            before = jnp.where(lane == 0, west, pltpu.roll(f, 1, 1))
            after = jnp.where(lane == width - 1, east, pltpu.roll(f, width - 1, 1))
            staged[k] = r_in[k] - (centre * f - (down + up + after + before))
        outs[p].start()
    for out in outs:
        out.wait()


def stencil(arrays, done, first, block):
    field = arrays[0]
    count, rows, width = field.shape
    specs = [*[HBM] * 3, *[VMEM] * 3]
    arrays = [*[in_hbm(a) for a in arrays[:3]], *arrays[3:]]
    part = block * rows * width
    if done is not None:
        arrays = [*arrays, done]
        specs = [*specs, HBM]
    cube = pltpu.VMEM((block, rows, width), F32)
    return pl.pallas_call(
        functools.partial(stencil_kernel, lax.axis_size("row"), first),
        in_specs=specs,
        out_specs=HBM,
        out_shape=jax.ShapeDtypeStruct(field.shape, F32),
        scratch_shapes=[
            cube,
            cube,
            pltpu.VMEM((rows, width), F32),
            cube,
            *[pltpu.SemaphoreType.DMA((-(-block // PIECE),))] * 3,
            pltpu.SemaphoreType.DMA(()),
        ],
        input_output_aliases={} if done is None else {6: 0},
        cost_estimate=pl.CostEstimate(flops=8 * part, bytes_accessed=48 * part, transcendentals=0),
        compiler_params=SMALL,
    )(*arrays)


def tied(*values):
    return lax.optimization_barrier(values)


def body(field, right_side, kappa, fronts):
    rows, cols = lax.axis_size("row"), lax.axis_size("col")
    i, j = lax.axis_index("row"), lax.axis_index("col")
    col_bits, row_bits = cols.bit_length() - 1, rows.bit_length() - 1
    places = [("col", b, j) for b in range(col_bits)] + [("row", b, i) for b in range(row_bits)]
    top = len(places) - 1

    first_row, *others = tied(first_row_of(field), right_side, kappa)
    below = rotated(first_row, "row", -1)
    last_row, part, rim = interface(field, *others)
    above = rotated(last_row, "row", 1)
    product = first_product(part, below, rim, fronts)
    given = None
    for level in range(col_bits):
        if level == 1:
            product, above = tied(product, above)
        got = swapped(product, "col", level)
        if level == 1:
            above = inner_only(above)
            got, above = tied(got, above)
        last = level == col_bits - 1
        product, rim, given = next_product(level, last, product, got, rim, given, fronts)
    arrays = (field, right_side, kappa, above, below, given)
    residual, at = None, 0

    def beside(step, value, residual, at, send):
        left = field.shape[0] - at
        share = left if step == -top else min(SHARES.get(step, 0), left)
        if not share:
            return send(value), residual, at
        value, *rest = tied(value, *arrays[:2], *([] if residual is None else [residual]))
        got = send(value)
        residual = stencil((*rest[:2], *arrays[2:]), rest[2] if rest[2:] else None, at, share)
        got, residual = tied(got, residual)
        return got, residual, at + share

    for level in range(col_bits, top + 1):
        axis, bit, owner = places[level]
        lower = jnp.bitwise_and(jnp.right_shift(owner, bit), 1) == 0
        got, residual, at = beside(
            level - top, product, residual, at, lambda v: swapped(v, axis, bit)
        )
        if level < top:
            state = jnp.where(lower, product + got, got - product)
            product = times_front(state, fronts[level + 1])
        else:
            state = times_front_t(got + got, fronts[level])
    for level in range(top - 1, -1, -1):
        axis, bit, owner = places[level]
        lower = jnp.bitwise_and(jnp.right_shift(owner, bit), 1) == 0
        got, residual, at = beside(
            level - top, state, residual, at, lambda v: swapped(v, axis, bit)
        )
        state = times_front_t(jnp.where(lower, state - got, state + got), fronts[level])
    return residual, state


SHARES = {0: 6, -2: 12, -3: 6}


def solution(mesh):
    placed = (P(None, "row", "col"), P(None, "row", "col"), P("row", "col"), P(None, "row", "col"))
    return jax.shard_map(
        body,
        mesh=mesh,
        in_specs=placed,
        out_specs=(P(None, "row", "col"), P("row", "col")),
        check_vma=False,
    )
```

```python
import functools

import jax
import jax.numpy as jnp
from jax import lax
from jax.experimental import pallas as pl
from jax.experimental.pallas import tpu as pltpu
from jax.sharding import PartitionSpec as P

F32 = jnp.float32
BF16 = jnp.bfloat16
TILE = 8
LANES = 128
WEST_UNIT, EAST_UNIT = 0, 1


def is_lower(level):
    return jnp.bitwise_and(jnp.right_shift(lax.axis_index("col"), level), 1) == 0


def swapped(value, axis, bit):
    count = lax.axis_size(axis)
    return lax.ppermute(value, axis, [(s, s ^ (1 << bit)) for s in range(count)])


def rotated(value, axis, step):
    count = lax.axis_size(axis)
    return lax.ppermute(value, axis, [(s, (s + step) % count) for s in range(count)])


def times_front(value, front):
    return jnp.dot(value.astype(BF16), front, preferred_element_type=F32)


def times_front_t(value, front):
    return lax.dot_general(
        value.astype(BF16), front, (((1,), (1,)), ((), ())), preferred_element_type=F32
    )


def in_vmem(shape):
    return pltpu.VMEM(shape, F32)


def in_hbm(value):
    return pltpu.with_memory_space_constraint(value, pltpu.HBM)


VMEM = pl.BlockSpec(memory_space=pltpu.VMEM)
HBM = pl.BlockSpec(memory_space=pltpu.HBM)
SMALL = pltpu.CompilerParams(vmem_limit_bytes=6 * 2**20)


def first_row_kernel(field, out, sem):
    copy = pltpu.make_async_copy(field.at[:, 0, :], out, sem)
    copy.start()
    copy.wait()


def first_row_of(field):
    count, _, width = field.shape
    return pl.pallas_call(
        first_row_kernel,
        in_specs=[HBM],
        out_specs=VMEM,
        out_shape=in_vmem((count, width)),
        scratch_shapes=[pltpu.SemaphoreType.DMA(())],
        compiler_params=SMALL,
    )(in_hbm(field))


def interface_kernel(field, right, kappa, last_row, part, rim, ahead, k1, sems):
    count, rows, width = field.shape
    end = rows - 1
    copies = [
        pltpu.make_async_copy(kappa.at[pl.ds(end, 1), :], k1, sems.at[0]),
        pltpu.make_async_copy(right.at[:, end, :], ahead, sems.at[1]),
    ]
    for copy in copies:
        copy.start()
    row = lax.broadcasted_iota(jnp.int32, (rows, LANES), 0)
    lane = lax.broadcasted_iota(jnp.int32, (rows, LANES), 1)
    for k in range(count):
        first, last = field[k, :, :1], field[k, :, width - 1 :]
        spread = jnp.where(lane == row, first, jnp.where(lane == row + rows, last, 0.0))
        rim[k : k + 1, :] = jnp.sum(spread, axis=0, keepdims=True)
    lane = lax.broadcasted_iota(jnp.int32, (count, width), 1)
    edge = field[:, end, :]
    last_row[...] = edge
    before = jnp.where(lane == 0, 0.0, pltpu.roll(edge, 1, 1))
    after = jnp.where(lane == width - 1, 0.0, pltpu.roll(edge, width - 1, 1))
    near = field[:, end - 1, :] + after + before
    for copy in copies:
        copy.wait()
    part[...] = ahead[...] - ((4.0 + k1[...]) * edge - near)


def interface(field, right_side, kappa):
    count, _, width = field.shape
    return pl.pallas_call(
        interface_kernel,
        in_specs=[VMEM, HBM, HBM],
        out_specs=[VMEM] * 3,
        out_shape=[in_vmem((count, width))] * 2 + [in_vmem((count, LANES))],
        scratch_shapes=[
            pltpu.VMEM((count, width), F32),
            pltpu.VMEM((1, width), F32),
            pltpu.SemaphoreType.DMA((2,)),
        ],
        compiler_params=SMALL,
    )(pltpu.with_memory_space_constraint(field, pltpu.VMEM), in_hbm(right_side), in_hbm(kappa))


def tiles_of(width):
    return width // LANES


def message_rows(count, width):
    return (count + 2) * tiles_of(width) + count // 2


def tile_at(t, l, width):
    return pl.ds((t * tiles_of(width) + l) * TILE, TILE)


def put_product(message, product, count, width):
    for t in range(count // TILE):
        for l in range(tiles_of(width)):
            tile = product[t * TILE : (t + 1) * TILE, l * LANES : (l + 1) * LANES]
            message[tile_at(t, l, width), :] = tile


def put_unit(message, which, unit, count, width):
    for l in range(tiles_of(width)):
        at = (count + which) * tiles_of(width) + l
        message[at : at + 1, :] = unit[:, l * LANES : (l + 1) * LANES]


def get_unit(message, which, count, width):
    at = (count + which) * tiles_of(width)
    return jnp.concatenate([message[at + l : at + l + 1, :] for l in range(tiles_of(width))], axis=1)


def put_rim(message, rim):
    at, half = message.shape[0] - rim.shape[0] // 2, rim.shape[0] // 2
    lane = lax.broadcasted_iota(jnp.int32, (half, LANES), 1)
    message[at:, :] = jnp.where(lane < LANES // 2, rim[:half], pltpu.roll(rim[half:], LANES // 2, 1))


def get_rim(message, count):
    piece = message[message.shape[0] - count // 2 :, :]
    return jnp.concatenate([piece, pltpu.roll(piece, LANES // 2, 1)], axis=0)


def first_product_kernel(has_rows, part, below, rim, fronts, message):
    count, width = part.shape
    has_below = lax.axis_index("row") < has_rows - 1
    state = part[...] + jnp.where(has_below, below[...], 0.0)
    product = jnp.dot(state.astype(BF16), fronts[0], preferred_element_type=F32)
    put_product(message, product, count, width)
    put_unit(message, WEST_UNIT, fronts[0, :16, :].astype(F32)[:1], count, width)
    put_unit(message, EAST_UNIT, fronts[0, width - 16 :, :].astype(F32)[15:], count, width)
    put_rim(message, rim[...])


def first_product(part, below, rim, fronts):
    count, width = part.shape
    return pl.pallas_call(
        functools.partial(first_product_kernel, lax.axis_size("row")),
        in_specs=[VMEM] * 4,
        out_specs=VMEM,
        out_shape=in_vmem((message_rows(count, width), LANES)),
        compiler_params=SMALL,
    )(part, below, rim, fronts)


def next_product_kernel(level, last, mine, theirs, rim, given, fronts, out, *rest):
    next_given = rest[-1]
    count, width = rim.shape[0], fronts.shape[1]
    rows = LANES // 4
    lower = is_lower(level)
    ones = 2**level - 1
    within = jnp.bitwise_and(lax.axis_index("col"), ones)
    lane = lax.broadcasted_iota(jnp.int32, (count, LANES), 1)
    own, other = rim[...], get_rim(theirs, count)
    takes_left = jnp.logical_and(jnp.logical_not(lower), within == 0)
    takes_right = jnp.logical_and(lower, within == ones)
    left, right = lane < rows, jnp.bitwise_and(lane, 3 * rows) == rows
    kept = jnp.zeros(other.shape, F32) if given is None else given[...]
    from_right = jnp.where(right, pltpu.roll(other, rows, 1), kept)
    kept = jnp.where(takes_right, from_right, kept)
    from_left = jnp.where(left, pltpu.roll(other, LANES - rows, 1), kept)
    next_given[...] = jnp.where(takes_left, from_left, kept)

    my_west, my_east = (get_unit(mine, u, count, width) for u in (WEST_UNIT, EAST_UNIT))
    their_west, their_east = (get_unit(theirs, u, count, width) for u in (WEST_UNIT, EAST_UNIT))
    into_mine = jnp.where(lower, other[:, rows - 1 : rows], -other[:, 2 * rows - 1 : 2 * rows])
    into_theirs = jnp.where(lower, own[:, 2 * rows - 1 : 2 * rows], own[:, rows - 1 : rows])
    my_unit = jnp.where(lower, my_east, my_west)
    their_unit = jnp.where(lower, their_west, their_east)

    def total(t, l):
        at = tile_at(t, l, width)
        return jnp.where(lower, theirs[at, :] + mine[at, :], theirs[at, :] - mine[at, :])

    downs, acrosses = range(count // TILE), range(tiles_of(width))
    state = [jnp.concatenate([total(t, l) for l in acrosses], axis=1) for t in downs]
    row = lax.broadcasted_iota(jnp.int32, (2 * TILE, width), 0)
    units = jnp.where(row == 0, my_unit, jnp.where(row == 1, their_unit, 0.0))
    if not last:
        west_unit = jnp.where(lower, my_west, their_west)
        east_unit = jnp.where(lower, their_east, -my_east)
        units = jnp.where(row == 2, west_unit, jnp.where(row == 3, east_unit, units))
    rows_in = jnp.concatenate([*state, units], axis=0).astype(BF16)
    product = jnp.dot(rows_in, fronts[level + 1], preferred_element_type=F32)
    result = (
        product[:count]
        + into_mine * product[count : count + 1]
        + into_theirs * product[count + 1 : count + 2]
    )
    if last:
        out[...] = result
        return
    put_product(out, result, count, width)
    put_unit(out, WEST_UNIT, product[count + 2 : count + 3], count, width)
    put_unit(out, EAST_UNIT, product[count + 3 : count + 4], count, width)
    turn = jnp.where(lower, 0, rows)
    block = jnp.where(jnp.bitwise_and(lane + turn, rows) == 0, own, other)
    rest[0][...] = block
    put_rim(out, block)


def next_product(level, levels, mine, theirs, rim, given, fronts):
    count, width = rim.shape[0], fronts.shape[1]
    last = level == levels - 1
    columns = in_vmem((count, LANES))
    message = in_vmem((message_rows(count, width), LANES))
    shapes = [in_vmem((count, width)), columns] if last else [message, columns, columns]
    operands = [mine, theirs, rim, *([] if given is None else [given]), fronts]

    def kernel(*refs):
        inputs, others = refs[: len(operands)], refs[len(operands) :]
        if given is None:
            inputs = (*inputs[:3], None, *inputs[3:])
        next_product_kernel(level, last, *inputs, *others)

    out = pl.pallas_call(
        kernel,
        in_specs=[VMEM] * len(operands),
        out_specs=[VMEM] * len(shapes),
        out_shape=shapes,
        compiler_params=SMALL,
    )(*operands)
    return out if not last else (out[0], None, out[1])


def inner_only_kernel(above, out):
    out[...] = jnp.where(lax.axis_index("row") > 0, above[...], 0.0)


def inner_only(above):
    return pl.pallas_call(
        inner_only_kernel,
        in_specs=[VMEM],
        out_specs=VMEM,
        out_shape=in_vmem(above.shape),
        cost_estimate=pl.CostEstimate(flops=above.size, bytes_accessed=2**24, transcendentals=0),
        compiler_params=SMALL,
    )(above)


PIECE = 4


def stencil_kernel(has_rows, first, field, right, kappa, above, below, given, *rest):
    done, f_in, r_in, k_in, staged, f_sems, r_sems, out_sems, k_sem = rest[-9:]
    block, rows, width = staged.shape
    starts = range(0, block, PIECE)
    fields, rights, outs = [], [], []
    for p, at in enumerate(starts):
        size = min(PIECE, block - at)
        here, there = pl.ds(at, size), pl.ds(first + at, size)
        fields.append(pltpu.make_async_copy(field.at[there], f_in.at[here], f_sems.at[p]))
        rights.append(pltpu.make_async_copy(right.at[there], r_in.at[here], r_sems.at[p]))
        outs.append(pltpu.make_async_copy(staged.at[here], done.at[there], out_sems.at[p]))
    kappa_in = pltpu.make_async_copy(kappa, k_in, k_sem)
    kappa_in.start()
    for f_copy, r_copy in zip(fields, rights):
        f_copy.start()
        r_copy.start()
    row = lax.broadcasted_iota(jnp.int32, (rows, width), 0)
    lane = lax.broadcasted_iota(jnp.int32, (rows, width), 1)
    cells = jnp.transpose(given[...])
    has_below = lax.axis_index("row") < has_rows - 1
    kappa_in.wait()
    centre = 4.0 + k_in[...]
    for p, at in enumerate(starts):
        fields[p].wait()
        rights[p].wait()
        for k in range(at, min(at + PIECE, block)):
            line = slice(first + k, first + k + 1)
            f = f_in[k]
            bottom = jnp.where(has_below, below[line, :], 0.0)
            up = jnp.where(row == 0, above[line, :], pltpu.roll(f, 1, 0))
            down = jnp.where(row == rows - 1, bottom, pltpu.roll(f, rows - 1, 0))
            west, east = cells[:rows, line], cells[rows : 2 * rows, line]
            before = jnp.where(lane == 0, west, pltpu.roll(f, 1, 1))
            after = jnp.where(lane == width - 1, east, pltpu.roll(f, width - 1, 1))
            staged[k] = r_in[k] - (centre * f - (down + up + after + before))
        outs[p].start()
    for out in outs:
        out.wait()


def stencil(arrays, done, first, block):
    field = arrays[0]
    count, rows, width = field.shape
    specs = [*[HBM] * 3, *[VMEM] * 3]
    arrays = [*[in_hbm(a) for a in arrays[:3]], *arrays[3:]]
    part = block * rows * width
    if done is not None:
        arrays = [*arrays, done]
        specs = [*specs, HBM]
    cube = pltpu.VMEM((block, rows, width), F32)
    return pl.pallas_call(
        functools.partial(stencil_kernel, lax.axis_size("row"), first),
        in_specs=specs,
        out_specs=HBM,
        out_shape=jax.ShapeDtypeStruct(field.shape, F32),
        scratch_shapes=[
            cube,
            cube,
            pltpu.VMEM((rows, width), F32),
            cube,
            *[pltpu.SemaphoreType.DMA((-(-block // PIECE),))] * 3,
            pltpu.SemaphoreType.DMA(()),
        ],
        input_output_aliases={} if done is None else {6: 0},
        cost_estimate=pl.CostEstimate(flops=8 * part, bytes_accessed=48 * part, transcendentals=0),
        compiler_params=SMALL,
    )(*arrays)


def tied(*values):
    return lax.optimization_barrier(values)


def body(field, right_side, kappa, fronts):
    rows, cols = lax.axis_size("row"), lax.axis_size("col")
    i, j = lax.axis_index("row"), lax.axis_index("col")
    col_bits, row_bits = cols.bit_length() - 1, rows.bit_length() - 1
    places = [("col", b, j) for b in range(col_bits)] + [("row", b, i) for b in range(row_bits)]
    top = len(places) - 1

    first_row, *others = tied(first_row_of(field), right_side, kappa)
    below = rotated(first_row, "row", -1)
    last_row, part, rim = interface(field, *others)
    above = rotated(last_row, "row", 1)
    product = first_product(part, below, rim, fronts)
    given = None
    for level in range(col_bits):
        if level == 1:
            product, above = tied(product, above)
        got = swapped(product, "col", level)
        if level == 1:
            above = inner_only(above)
            got, above = tied(got, above)
        product, rim, given = next_product(level, col_bits, product, got, rim, given, fronts)
    arrays = (field, right_side, kappa, above, below, given)
    residual, at = None, 0

    def beside(step, value, residual, at, send):
        left = field.shape[0] - at
        share = left if step == -top else min(SHARES.get(step, 0), left)
        if not share:
            return send(value), residual, at
        value, *rest = tied(value, *arrays[:2], *([] if residual is None else [residual]))
        got = send(value)
        residual = stencil((*rest[:2], *arrays[2:]), rest[2] if rest[2:] else None, at, share)
        got, residual = tied(got, residual)
        return got, residual, at + share

    for level in range(col_bits, top + 1):
        axis, bit, owner = places[level]
        lower = jnp.bitwise_and(jnp.right_shift(owner, bit), 1) == 0
        got, residual, at = beside(
            level - top, product, residual, at, lambda v: swapped(v, axis, bit)
        )
        if level < top:
            state = jnp.where(lower, product + got, got - product)
            product = times_front(state, fronts[level + 1])
        else:
            state = times_front_t(got + got, fronts[level])
    for level in range(top - 1, -1, -1):
        axis, bit, owner = places[level]
        lower = jnp.bitwise_and(jnp.right_shift(owner, bit), 1) == 0
        got, residual, at = beside(
            level - top, state, residual, at, lambda v: swapped(v, axis, bit)
        )
        state = times_front_t(jnp.where(lower, state - got, state + got), fronts[level])
    return residual, state


SHARES = {0: 6, -2: 12, -3: 6}


def solution(mesh):
    placed = (P(None, "row", "col"), P(None, "row", "col"), P("row", "col"), P(None, "row", "col"))
    return jax.shard_map(
        body,
        mesh=mesh,
        in_specs=placed,
        out_specs=(P(None, "row", "col"), P("row", "col")),
        check_vma=False,
    )
```

```python
import functools

import jax
import jax.numpy as jnp
from jax import lax
from jax.experimental import pallas as pl
from jax.experimental.pallas import tpu as pltpu
from jax.sharding import PartitionSpec as P

F32 = jnp.float32
BF16 = jnp.bfloat16
TILE = 8
LANES = 128
WEST_UNIT, EAST_UNIT = 0, 1


def is_lower(level):
    return jnp.bitwise_and(jnp.right_shift(lax.axis_index("col"), level), 1) == 0


def swapped(value, axis, bit):
    count = lax.axis_size(axis)
    return lax.ppermute(value, axis, [(s, s ^ (1 << bit)) for s in range(count)])


def rotated(value, axis, step):
    count = lax.axis_size(axis)
    return lax.ppermute(value, axis, [(s, (s + step) % count) for s in range(count)])


def times_front(value, front):
    return jnp.dot(value.astype(BF16), front, preferred_element_type=F32)


def times_front_t(value, front):
    return lax.dot_general(
        value.astype(BF16), front, (((1,), (1,)), ((), ())), preferred_element_type=F32
    )


def in_vmem(shape):
    return pltpu.VMEM(shape, F32)


def in_hbm(value):
    return pltpu.with_memory_space_constraint(value, pltpu.HBM)


VMEM = pl.BlockSpec(memory_space=pltpu.VMEM)
HBM = pl.BlockSpec(memory_space=pltpu.HBM)
SMALL = pltpu.CompilerParams(vmem_limit_bytes=6 * 2**20)


def first_row_kernel(field, out, sem):
    copy = pltpu.make_async_copy(field.at[:, 0, :], out, sem)
    copy.start()
    copy.wait()


def first_row_of(field):
    count, _, width = field.shape
    return pl.pallas_call(
        first_row_kernel,
        in_specs=[HBM],
        out_specs=VMEM,
        out_shape=in_vmem((count, width)),
        scratch_shapes=[pltpu.SemaphoreType.DMA(())],
        compiler_params=SMALL,
    )(in_hbm(field))


def interface_kernel(field, right, kappa, last_row, part, rim, ahead, k1, sems):
    count, rows, width = field.shape
    end = rows - 1
    copies = [
        pltpu.make_async_copy(kappa.at[pl.ds(end, 1), :], k1, sems.at[0]),
        pltpu.make_async_copy(right.at[:, end, :], ahead, sems.at[1]),
    ]
    for copy in copies:
        copy.start()
    row = lax.broadcasted_iota(jnp.int32, (rows, LANES), 0)
    lane = lax.broadcasted_iota(jnp.int32, (rows, LANES), 1)
    for k in range(count):
        first, last = field[k, :, :1], field[k, :, width - 1 :]
        spread = jnp.where(lane == row, first, jnp.where(lane == row + rows, last, 0.0))
        rim[k : k + 1, :] = jnp.sum(spread, axis=0, keepdims=True)
    lane = lax.broadcasted_iota(jnp.int32, (count, width), 1)
    edge = field[:, end, :]
    last_row[...] = edge
    before = jnp.where(lane == 0, 0.0, pltpu.roll(edge, 1, 1))
    after = jnp.where(lane == width - 1, 0.0, pltpu.roll(edge, width - 1, 1))
    near = field[:, end - 1, :] + after + before
    for copy in copies:
        copy.wait()
    part[...] = ahead[...] - ((4.0 + k1[...]) * edge - near)


def interface(field, right_side, kappa):
    count, _, width = field.shape
    return pl.pallas_call(
        interface_kernel,
        in_specs=[VMEM, HBM, HBM],
        out_specs=[VMEM] * 3,
        out_shape=[in_vmem((count, width))] * 2 + [in_vmem((count, LANES))],
        scratch_shapes=[
            pltpu.VMEM((count, width), F32),
            pltpu.VMEM((1, width), F32),
            pltpu.SemaphoreType.DMA((2,)),
        ],
        compiler_params=SMALL,
    )(pltpu.with_memory_space_constraint(field, pltpu.VMEM), in_hbm(right_side), in_hbm(kappa))


def tiles_of(width):
    return width // LANES


def message_rows(count, width):
    return (count + 2) * tiles_of(width) + count // 2


def tile_at(t, l, width):
    return pl.ds((t * tiles_of(width) + l) * TILE, TILE)


def put_product(message, product, count, width):
    for t in range(count // TILE):
        for l in range(tiles_of(width)):
            tile = product[t * TILE : (t + 1) * TILE, l * LANES : (l + 1) * LANES]
            message[tile_at(t, l, width), :] = tile


def put_unit(message, which, unit, count, width):
    for l in range(tiles_of(width)):
        at = (count + which) * tiles_of(width) + l
        message[at : at + 1, :] = unit[:, l * LANES : (l + 1) * LANES]


def get_unit(message, which, count, width):
    at = (count + which) * tiles_of(width)
    return jnp.concatenate([message[at + l : at + l + 1, :] for l in range(tiles_of(width))], axis=1)


def put_rim(message, rim):
    at, half = message.shape[0] - rim.shape[0] // 2, rim.shape[0] // 2
    lane = lax.broadcasted_iota(jnp.int32, (half, LANES), 1)
    message[at:, :] = jnp.where(lane < LANES // 2, rim[:half], pltpu.roll(rim[half:], LANES // 2, 1))


def get_rim(message, count):
    piece = message[message.shape[0] - count // 2 :, :]
    return jnp.concatenate([piece, pltpu.roll(piece, LANES // 2, 1)], axis=0)


def first_product_kernel(has_rows, part, below, rim, fronts, message):
    count, width = part.shape
    has_below = lax.axis_index("row") < has_rows - 1
    state = part[...] + jnp.where(has_below, below[...], 0.0)
    product = jnp.dot(state.astype(BF16), fronts[0], preferred_element_type=F32)
    put_product(message, product, count, width)
    put_unit(message, WEST_UNIT, fronts[0, :16, :].astype(F32)[:1], count, width)
    put_unit(message, EAST_UNIT, fronts[0, width - 16 :, :].astype(F32)[15:], count, width)
    put_rim(message, rim[...])


def first_product(part, below, rim, fronts):
    count, width = part.shape
    return pl.pallas_call(
        functools.partial(first_product_kernel, lax.axis_size("row")),
        in_specs=[VMEM] * 4,
        out_specs=VMEM,
        out_shape=in_vmem((message_rows(count, width), LANES)),
        compiler_params=SMALL,
    )(part, below, rim, fronts)


def next_product_kernel(level, last, mine, theirs, rim, given, fronts, out, *rest):
    next_given = rest[-1]
    count, width = rim.shape[0], fronts.shape[1]
    rows = LANES // 4
    lower = is_lower(level)
    ones = 2**level - 1
    within = jnp.bitwise_and(lax.axis_index("col"), ones)
    lane = lax.broadcasted_iota(jnp.int32, (count, LANES), 1)
    own, other = rim[...], get_rim(theirs, count)
    takes_left = jnp.logical_and(jnp.logical_not(lower), within == 0)
    takes_right = jnp.logical_and(lower, within == ones)
    left, right = lane < rows, jnp.bitwise_and(lane, 3 * rows) == rows
    kept = jnp.zeros(other.shape, F32) if given is None else given[...]
    from_right = jnp.where(right, pltpu.roll(other, rows, 1), kept)
    kept = jnp.where(takes_right, from_right, kept)
    from_left = jnp.where(left, pltpu.roll(other, LANES - rows, 1), kept)
    next_given[...] = jnp.where(takes_left, from_left, kept)

    my_west, my_east = (get_unit(mine, u, count, width) for u in (WEST_UNIT, EAST_UNIT))
    their_west, their_east = (get_unit(theirs, u, count, width) for u in (WEST_UNIT, EAST_UNIT))
    into_mine = jnp.where(lower, other[:, rows - 1 : rows], -other[:, 2 * rows - 1 : 2 * rows])
    into_theirs = jnp.where(lower, own[:, 2 * rows - 1 : 2 * rows], own[:, rows - 1 : rows])
    my_unit = jnp.where(lower, my_east, my_west)
    their_unit = jnp.where(lower, their_west, their_east)

    def total(t, l):
        at = tile_at(t, l, width)
        return jnp.where(lower, theirs[at, :] + mine[at, :], theirs[at, :] - mine[at, :])

    downs, acrosses = range(count // TILE), range(tiles_of(width))
    state = [jnp.concatenate([total(t, l) for l in acrosses], axis=1) for t in downs]
    row = lax.broadcasted_iota(jnp.int32, (2 * TILE, width), 0)
    units = jnp.where(row == 0, my_unit, jnp.where(row == 1, their_unit, 0.0))
    if not last:
        west_unit = jnp.where(lower, my_west, their_west)
        east_unit = jnp.where(lower, their_east, -my_east)
        units = jnp.where(row == 2, west_unit, jnp.where(row == 3, east_unit, units))
    rows_in = jnp.concatenate([*state, units], axis=0).astype(BF16)
    product = jnp.dot(rows_in, fronts[level + 1], preferred_element_type=F32)
    result = (
        product[:count]
        + into_mine * product[count : count + 1]
        + into_theirs * product[count + 1 : count + 2]
    )
    if last:
        out[...] = result
        return
    put_product(out, result, count, width)
    put_unit(out, WEST_UNIT, product[count + 2 : count + 3], count, width)
    put_unit(out, EAST_UNIT, product[count + 3 : count + 4], count, width)
    turn = jnp.where(lower, 0, rows)
    block = jnp.where(jnp.bitwise_and(lane + turn, rows) == 0, own, other)
    rest[0][...] = block
    put_rim(out, block)


def next_product(level, levels, mine, theirs, rim, given, fronts):
    count, width = rim.shape[0], fronts.shape[1]
    last = level == levels - 1
    columns = in_vmem((count, LANES))
    message = in_vmem((message_rows(count, width), LANES))
    shapes = [in_vmem((count, width)), columns] if last else [message, columns, columns]
    operands = [mine, theirs, rim, *([] if given is None else [given]), fronts]

    def kernel(*refs):
        inputs, others = refs[: len(operands)], refs[len(operands) :]
        if given is None:
            inputs = (*inputs[:3], None, *inputs[3:])
        next_product_kernel(level, last, *inputs, *others)

    out = pl.pallas_call(
        kernel,
        in_specs=[VMEM] * len(operands),
        out_specs=[VMEM] * len(shapes),
        out_shape=shapes,
        compiler_params=SMALL,
    )(*operands)
    return out if not last else (out[0], None, out[1])


def inner_only_kernel(above, out):
    out[...] = jnp.where(lax.axis_index("row") > 0, above[...], 0.0)


def inner_only(above):
    return pl.pallas_call(
        inner_only_kernel,
        in_specs=[VMEM],
        out_specs=VMEM,
        out_shape=in_vmem(above.shape),
        cost_estimate=pl.CostEstimate(flops=above.size, bytes_accessed=2**24, transcendentals=0),
        compiler_params=SMALL,
    )(above)


PIECE = 4


def stencil_kernel(has_rows, first, field, right, kappa, above, below, given, *rest):
    done, f_in, r_in, k_in, staged, f_sems, r_sems, out_sems, k_sem = rest[-9:]
    block, rows, width = staged.shape
    starts = range(0, block, PIECE)
    fields, rights, outs = [], [], []
    for p, at in enumerate(starts):
        size = min(PIECE, block - at)
        here, there = pl.ds(at, size), pl.ds(first + at, size)
        fields.append(pltpu.make_async_copy(field.at[there], f_in.at[here], f_sems.at[p]))
        rights.append(pltpu.make_async_copy(right.at[there], r_in.at[here], r_sems.at[p]))
        outs.append(pltpu.make_async_copy(staged.at[here], done.at[there], out_sems.at[p]))
    kappa_in = pltpu.make_async_copy(kappa, k_in, k_sem)
    kappa_in.start()
    for f_copy, r_copy in zip(fields, rights):
        f_copy.start()
        r_copy.start()
    row = lax.broadcasted_iota(jnp.int32, (rows, width), 0)
    lane = lax.broadcasted_iota(jnp.int32, (rows, width), 1)
    cells = jnp.transpose(given[...])
    has_below = lax.axis_index("row") < has_rows - 1
    kappa_in.wait()
    centre = 4.0 + k_in[...]
    for p, at in enumerate(starts):
        fields[p].wait()
        rights[p].wait()
        for k in range(at, min(at + PIECE, block)):
            line = slice(first + k, first + k + 1)
            f = f_in[k]
            bottom = jnp.where(has_below, below[line, :], 0.0)
            up = jnp.where(row == 0, above[line, :], pltpu.roll(f, 1, 0))
            down = jnp.where(row == rows - 1, bottom, pltpu.roll(f, rows - 1, 0))
            west, east = cells[:rows, line], cells[rows : 2 * rows, line]
            before = jnp.where(lane == 0, west, pltpu.roll(f, 1, 1))
            after = jnp.where(lane == width - 1, east, pltpu.roll(f, width - 1, 1))
            staged[k] = r_in[k] - (centre * f - (down + up + after + before))
        outs[p].start()
    for out in outs:
        out.wait()


def stencil(arrays, done, first, block):
    field = arrays[0]
    count, rows, width = field.shape
    specs = [*[HBM] * 3, *[VMEM] * 3]
    arrays = [*[in_hbm(a) for a in arrays[:3]], *arrays[3:]]
    part = block * rows * width
    if done is not None:
        arrays = [*arrays, done]
        specs = [*specs, HBM]
    cube = pltpu.VMEM((block, rows, width), F32)
    return pl.pallas_call(
        functools.partial(stencil_kernel, lax.axis_size("row"), first),
        in_specs=specs,
        out_specs=HBM,
        out_shape=jax.ShapeDtypeStruct(field.shape, F32),
        scratch_shapes=[
            cube,
            cube,
            pltpu.VMEM((rows, width), F32),
            cube,
            *[pltpu.SemaphoreType.DMA((-(-block // PIECE),))] * 3,
            pltpu.SemaphoreType.DMA(()),
        ],
        input_output_aliases={} if done is None else {6: 0},
        cost_estimate=pl.CostEstimate(flops=8 * part, bytes_accessed=48 * part, transcendentals=0),
        compiler_params=SMALL,
    )(*arrays)


def turn_kernel(levels, fronts, *out):
    for level, to in zip(levels, out):
        to[...] = jnp.transpose(fronts[level])


def turned(fronts, levels):
    shape = jax.ShapeDtypeStruct(fronts.shape[1:], fronts.dtype)
    return pl.pallas_call(
        functools.partial(turn_kernel, levels),
        in_specs=[VMEM],
        out_specs=[VMEM] * len(levels),
        out_shape=[shape] * len(levels),
        cost_estimate=pl.CostEstimate(flops=0, bytes_accessed=2**23, transcendentals=0),
        compiler_params=SMALL,
    )(fronts)


def tied(*values):
    return lax.optimization_barrier(values)


def body(field, right_side, kappa, fronts):
    rows, cols = lax.axis_size("row"), lax.axis_size("col")
    i, j = lax.axis_index("row"), lax.axis_index("col")
    col_bits, row_bits = cols.bit_length() - 1, rows.bit_length() - 1
    places = [("col", b, j) for b in range(col_bits)] + [("row", b, i) for b in range(row_bits)]
    top = len(places) - 1

    first_row, *others = tied(first_row_of(field), right_side, kappa)
    below = rotated(first_row, "row", -1)
    last_row, part, rim = interface(field, *others)
    above = rotated(last_row, "row", 1)
    product = first_product(part, below, rim, fronts)
    given, flipped = None, {}
    plan = {1: (top, top - 1), 2: (2, 1, 0)}
    for level in range(col_bits):
        if level == 1:
            product, above = tied(product, above)
        levels = plan.get(level, ())
        if levels:
            product, fronts_in = tied(product, fronts)
        got = swapped(product, "col", level)
        if levels:
            got, *backs = tied(got, *turned(fronts_in, levels))
            flipped.update(zip(levels, backs))
        if level == 1:
            above = inner_only(above)
            got, above = tied(got, above)
        product, rim, given = next_product(level, col_bits, product, got, rim, given, fronts)
    arrays = (field, right_side, kappa, above, below, given)
    residual, at = None, 0

    def back_product(value, level):
        if level in flipped:
            return times_front(value, flipped[level])
        return times_front_t(value, fronts[level])

    def beside(step, value, residual, at, send):
        left = field.shape[0] - at
        share = left if step == -top else min(SHARES.get(step, 0), left)
        if not share:
            return send(value), residual, at
        value, *rest = tied(value, *arrays[:2], *([] if residual is None else [residual]))
        got = send(value)
        residual = stencil((*rest[:2], *arrays[2:]), rest[2] if rest[2:] else None, at, share)
        got, residual = tied(got, residual)
        return got, residual, at + share

    for level in range(col_bits, top + 1):
        axis, bit, owner = places[level]
        lower = jnp.bitwise_and(jnp.right_shift(owner, bit), 1) == 0
        got, residual, at = beside(
            level - top, product, residual, at, lambda v: swapped(v, axis, bit)
        )
        if level < top:
            state = jnp.where(lower, product + got, got - product)
            product = times_front(state, fronts[level + 1])
        else:
            state = back_product(got + got, level)
    for level in range(top - 1, -1, -1):
        axis, bit, owner = places[level]
        lower = jnp.bitwise_and(jnp.right_shift(owner, bit), 1) == 0
        got, residual, at = beside(
            level - top, state, residual, at, lambda v: swapped(v, axis, bit)
        )
        state = back_product(jnp.where(lower, state - got, state + got), level)
    return residual, state


SHARES = {0: 6, -2: 12, -3: 6}


def solution(mesh):
    placed = (P(None, "row", "col"), P(None, "row", "col"), P("row", "col"), P(None, "row", "col"))
    return jax.shard_map(
        body,
        mesh=mesh,
        in_specs=placed,
        out_specs=(P(None, "row", "col"), P("row", "col")),
        check_vma=False,
    )
```

```python
import functools

import jax
import jax.numpy as jnp
from jax import lax
from jax.experimental import pallas as pl
from jax.experimental.pallas import tpu as pltpu
from jax.sharding import PartitionSpec as P

F32 = jnp.float32
BF16 = jnp.bfloat16
TILE = 8
LANES = 128
WEST_UNIT, EAST_UNIT = 0, 1


def is_lower(level):
    return jnp.bitwise_and(jnp.right_shift(lax.axis_index("col"), level), 1) == 0


def swapped(value, axis, bit):
    count = lax.axis_size(axis)
    return lax.ppermute(value, axis, [(s, s ^ (1 << bit)) for s in range(count)])


def rotated(value, axis, step):
    count = lax.axis_size(axis)
    return lax.ppermute(value, axis, [(s, (s + step) % count) for s in range(count)])


def times_front(value, front):
    return jnp.dot(value.astype(BF16), front, preferred_element_type=F32)


def times_front_t(value, front):
    return lax.dot_general(
        value.astype(BF16), front, (((1,), (1,)), ((), ())), preferred_element_type=F32
    )


def in_vmem(shape):
    return pltpu.VMEM(shape, F32)


def in_hbm(value):
    return pltpu.with_memory_space_constraint(value, pltpu.HBM)


VMEM = pl.BlockSpec(memory_space=pltpu.VMEM)
HBM = pl.BlockSpec(memory_space=pltpu.HBM)
SMALL = pltpu.CompilerParams(vmem_limit_bytes=6 * 2**20)


def first_row_kernel(field, out, sem):
    copy = pltpu.make_async_copy(field.at[:, 0, :], out, sem)
    copy.start()
    copy.wait()


def first_row_of(field):
    count, _, width = field.shape
    return pl.pallas_call(
        first_row_kernel,
        in_specs=[HBM],
        out_specs=VMEM,
        out_shape=in_vmem((count, width)),
        scratch_shapes=[pltpu.SemaphoreType.DMA(())],
        compiler_params=SMALL,
    )(in_hbm(field))


def interface_kernel(field, right, kappa, last_row, part, rim, ahead, k1, sems):
    count, rows, width = field.shape
    end = rows - 1
    copies = [
        pltpu.make_async_copy(kappa.at[pl.ds(end, 1), :], k1, sems.at[0]),
        pltpu.make_async_copy(right.at[:, end, :], ahead, sems.at[1]),
    ]
    for copy in copies:
        copy.start()
    row = lax.broadcasted_iota(jnp.int32, (rows, LANES), 0)
    lane = lax.broadcasted_iota(jnp.int32, (rows, LANES), 1)
    for k in range(count):
        first, last = field[k, :, :1], field[k, :, width - 1 :]
        spread = jnp.where(lane == row, first, jnp.where(lane == row + rows, last, 0.0))
        rim[k : k + 1, :] = jnp.sum(spread, axis=0, keepdims=True)
    lane = lax.broadcasted_iota(jnp.int32, (count, width), 1)
    edge = field[:, end, :]
    last_row[...] = edge
    before = jnp.where(lane == 0, 0.0, pltpu.roll(edge, 1, 1))
    after = jnp.where(lane == width - 1, 0.0, pltpu.roll(edge, width - 1, 1))
    near = field[:, end - 1, :] + after + before
    for copy in copies:
        copy.wait()
    part[...] = ahead[...] - ((4.0 + k1[...]) * edge - near)


def interface(field, right_side, kappa):
    count, _, width = field.shape
    return pl.pallas_call(
        interface_kernel,
        in_specs=[VMEM, HBM, HBM],
        out_specs=[VMEM] * 3,
        out_shape=[in_vmem((count, width))] * 2 + [in_vmem((count, LANES))],
        scratch_shapes=[
            pltpu.VMEM((count, width), F32),
            pltpu.VMEM((1, width), F32),
            pltpu.SemaphoreType.DMA((2,)),
        ],
        compiler_params=SMALL,
    )(pltpu.with_memory_space_constraint(field, pltpu.VMEM), in_hbm(right_side), in_hbm(kappa))


def tiles_of(width):
    return width // LANES


def message_rows(count, width):
    return (count + 2) * tiles_of(width) + count // 2


def tile_at(t, l, width):
    return pl.ds((t * tiles_of(width) + l) * TILE, TILE)


def put_product(message, product, count, width):
    for t in range(count // TILE):
        for l in range(tiles_of(width)):
            tile = product[t * TILE : (t + 1) * TILE, l * LANES : (l + 1) * LANES]
            message[tile_at(t, l, width), :] = tile


def put_unit(message, which, unit, count, width):
    for l in range(tiles_of(width)):
        at = (count + which) * tiles_of(width) + l
        message[at : at + 1, :] = unit[:, l * LANES : (l + 1) * LANES]


def get_unit(message, which, count, width):
    at = (count + which) * tiles_of(width)
    return jnp.concatenate([message[at + l : at + l + 1, :] for l in range(tiles_of(width))], axis=1)


def put_rim(message, rim):
    at, half = message.shape[0] - rim.shape[0] // 2, rim.shape[0] // 2
    lane = lax.broadcasted_iota(jnp.int32, (half, LANES), 1)
    message[at:, :] = jnp.where(lane < LANES // 2, rim[:half], pltpu.roll(rim[half:], LANES // 2, 1))


def get_rim(message, count):
    piece = message[message.shape[0] - count // 2 :, :]
    return jnp.concatenate([piece, pltpu.roll(piece, LANES // 2, 1)], axis=0)


def first_product_kernel(has_rows, part, below, rim, fronts, message):
    count, width = part.shape
    has_below = lax.axis_index("row") < has_rows - 1
    state = part[...] + jnp.where(has_below, below[...], 0.0)
    product = jnp.dot(state.astype(BF16), fronts[0], preferred_element_type=F32)
    put_product(message, product, count, width)
    put_unit(message, WEST_UNIT, fronts[0, :16, :].astype(F32)[:1], count, width)
    put_unit(message, EAST_UNIT, fronts[0, width - 16 :, :].astype(F32)[15:], count, width)
    put_rim(message, rim[...])


def first_product(part, below, rim, fronts):
    count, width = part.shape
    return pl.pallas_call(
        functools.partial(first_product_kernel, lax.axis_size("row")),
        in_specs=[VMEM] * 4,
        out_specs=VMEM,
        out_shape=in_vmem((message_rows(count, width), LANES)),
        compiler_params=SMALL,
    )(part, below, rim, fronts)


def next_product_kernel(level, last, mine, theirs, rim, given, fronts, out, *rest):
    next_given = rest[-1]
    count, width = rim.shape[0], fronts.shape[1]
    rows = LANES // 4
    lower = is_lower(level)
    ones = 2**level - 1
    within = jnp.bitwise_and(lax.axis_index("col"), ones)
    lane = lax.broadcasted_iota(jnp.int32, (count, LANES), 1)
    own, other = rim[...], get_rim(theirs, count)
    takes_left = jnp.logical_and(jnp.logical_not(lower), within == 0)
    takes_right = jnp.logical_and(lower, within == ones)
    left, right = lane < rows, jnp.bitwise_and(lane, 3 * rows) == rows
    kept = jnp.zeros(other.shape, F32) if given is None else given[...]
    from_right = jnp.where(right, pltpu.roll(other, rows, 1), kept)
    kept = jnp.where(takes_right, from_right, kept)
    from_left = jnp.where(left, pltpu.roll(other, LANES - rows, 1), kept)
    next_given[...] = jnp.where(takes_left, from_left, kept)

    my_west, my_east = (get_unit(mine, u, count, width) for u in (WEST_UNIT, EAST_UNIT))
    their_west, their_east = (get_unit(theirs, u, count, width) for u in (WEST_UNIT, EAST_UNIT))
    into_mine = jnp.where(lower, other[:, rows - 1 : rows], -other[:, 2 * rows - 1 : 2 * rows])
    into_theirs = jnp.where(lower, own[:, 2 * rows - 1 : 2 * rows], own[:, rows - 1 : rows])
    my_unit = jnp.where(lower, my_east, my_west)
    their_unit = jnp.where(lower, their_west, their_east)

    def total(t, l):
        at = tile_at(t, l, width)
        return jnp.where(lower, theirs[at, :] + mine[at, :], theirs[at, :] - mine[at, :])

    downs, acrosses = range(count // TILE), range(tiles_of(width))
    state = [jnp.concatenate([total(t, l) for l in acrosses], axis=1) for t in downs]
    row = lax.broadcasted_iota(jnp.int32, (2 * TILE, width), 0)
    units = jnp.where(row == 0, my_unit, jnp.where(row == 1, their_unit, 0.0))
    if not last:
        west_unit = jnp.where(lower, my_west, their_west)
        east_unit = jnp.where(lower, their_east, -my_east)
        units = jnp.where(row == 2, west_unit, jnp.where(row == 3, east_unit, units))
    rows_in = jnp.concatenate([*state, units], axis=0).astype(BF16)
    product = jnp.dot(rows_in, fronts[level + 1], preferred_element_type=F32)
    result = (
        product[:count]
        + into_mine * product[count : count + 1]
        + into_theirs * product[count + 1 : count + 2]
    )
    if last:
        out[...] = result
        return
    put_product(out, result, count, width)
    put_unit(out, WEST_UNIT, product[count + 2 : count + 3], count, width)
    put_unit(out, EAST_UNIT, product[count + 3 : count + 4], count, width)
    turn = jnp.where(lower, 0, rows)
    block = jnp.where(jnp.bitwise_and(lane + turn, rows) == 0, own, other)
    rest[0][...] = block
    put_rim(out, block)


def next_product(level, levels, mine, theirs, rim, given, fronts):
    count, width = rim.shape[0], fronts.shape[1]
    last = level == levels - 1
    columns = in_vmem((count, LANES))
    message = in_vmem((message_rows(count, width), LANES))
    shapes = [in_vmem((count, width)), columns] if last else [message, columns, columns]
    operands = [mine, theirs, rim, *([] if given is None else [given]), fronts]

    def kernel(*refs):
        inputs, others = refs[: len(operands)], refs[len(operands) :]
        if given is None:
            inputs = (*inputs[:3], None, *inputs[3:])
        next_product_kernel(level, last, *inputs, *others)

    out = pl.pallas_call(
        kernel,
        in_specs=[VMEM] * len(operands),
        out_specs=[VMEM] * len(shapes),
        out_shape=shapes,
        compiler_params=SMALL,
    )(*operands)
    return out if not last else (out[0], None, out[1])


def inner_only_kernel(above, out):
    out[...] = jnp.where(lax.axis_index("row") > 0, above[...], 0.0)


def inner_only(above):
    return pl.pallas_call(
        inner_only_kernel,
        in_specs=[VMEM],
        out_specs=VMEM,
        out_shape=in_vmem(above.shape),
        cost_estimate=pl.CostEstimate(flops=above.size, bytes_accessed=2**24, transcendentals=0),
        compiler_params=SMALL,
    )(above)


PIECE = 4


def stencil_kernel(has_rows, first, field, right, kappa, above, below, given, *rest):
    done, f_in, r_in, k_in, staged, f_sems, r_sems, out_sems, k_sem = rest[-9:]
    block, rows, width = staged.shape
    starts = range(0, block, PIECE)
    fields, rights, outs = [], [], []
    for p, at in enumerate(starts):
        size = min(PIECE, block - at)
        here, there = pl.ds(at, size), pl.ds(first + at, size)
        fields.append(pltpu.make_async_copy(field.at[there], f_in.at[here], f_sems.at[p]))
        rights.append(pltpu.make_async_copy(right.at[there], r_in.at[here], r_sems.at[p]))
        outs.append(pltpu.make_async_copy(staged.at[here], done.at[there], out_sems.at[p]))
    kappa_in = pltpu.make_async_copy(kappa, k_in, k_sem)
    kappa_in.start()
    for f_copy, r_copy in zip(fields, rights):
        f_copy.start()
        r_copy.start()
    row = lax.broadcasted_iota(jnp.int32, (rows, width), 0)
    lane = lax.broadcasted_iota(jnp.int32, (rows, width), 1)
    cells = jnp.transpose(given[...])
    has_below = lax.axis_index("row") < has_rows - 1
    kappa_in.wait()
    centre = 4.0 + k_in[...]
    for p, at in enumerate(starts):
        fields[p].wait()
        rights[p].wait()
        for k in range(at, min(at + PIECE, block)):
            line = slice(first + k, first + k + 1)
            f = f_in[k]
            bottom = jnp.where(has_below, below[line, :], 0.0)
            up = jnp.where(row == 0, above[line, :], pltpu.roll(f, 1, 0))
            down = jnp.where(row == rows - 1, bottom, pltpu.roll(f, rows - 1, 0))
            west, east = cells[:rows, line], cells[rows : 2 * rows, line]
            before = jnp.where(lane == 0, west, pltpu.roll(f, 1, 1))
            after = jnp.where(lane == width - 1, east, pltpu.roll(f, width - 1, 1))
            staged[k] = r_in[k] - (centre * f - (down + up + after + before))
        outs[p].start()
    for out in outs:
        out.wait()


def stencil(arrays, done, first, block):
    field = arrays[0]
    count, rows, width = field.shape
    specs = [*[HBM] * 3, *[VMEM] * 3]
    arrays = [*[in_hbm(a) for a in arrays[:3]], *arrays[3:]]
    part = block * rows * width
    if done is not None:
        arrays = [*arrays, done]
        specs = [*specs, HBM]
    cube = pltpu.VMEM((block, rows, width), F32)
    return pl.pallas_call(
        functools.partial(stencil_kernel, lax.axis_size("row"), first),
        in_specs=specs,
        out_specs=HBM,
        out_shape=jax.ShapeDtypeStruct(field.shape, F32),
        scratch_shapes=[
            cube,
            cube,
            pltpu.VMEM((rows, width), F32),
            cube,
            *[pltpu.SemaphoreType.DMA((-(-block // PIECE),))] * 3,
            pltpu.SemaphoreType.DMA(()),
        ],
        input_output_aliases={} if done is None else {6: 0},
        cost_estimate=pl.CostEstimate(flops=8 * part, bytes_accessed=48 * part, transcendentals=0),
        compiler_params=SMALL,
    )(*arrays)


def turn_kernel(levels, fronts, *out):
    for level, to in zip(levels, out):
        to[...] = jnp.transpose(fronts[level])


def turned(fronts, levels):
    shape = jax.ShapeDtypeStruct(fronts.shape[1:], fronts.dtype)
    return pl.pallas_call(
        functools.partial(turn_kernel, levels),
        in_specs=[VMEM],
        out_specs=[VMEM] * len(levels),
        out_shape=[shape] * len(levels),
        cost_estimate=pl.CostEstimate(flops=0, bytes_accessed=2**23, transcendentals=0),
        compiler_params=SMALL,
    )(fronts)


def tied(*values):
    return lax.optimization_barrier(values)


def body(field, right_side, kappa, fronts):
    rows, cols = lax.axis_size("row"), lax.axis_size("col")
    i, j = lax.axis_index("row"), lax.axis_index("col")
    col_bits, row_bits = cols.bit_length() - 1, rows.bit_length() - 1
    places = [("col", b, j) for b in range(col_bits)] + [("row", b, i) for b in range(row_bits)]
    top = len(places) - 1

    first_row, *others = tied(first_row_of(field), right_side, kappa)
    below = rotated(first_row, "row", -1)
    last_row, part, rim = interface(field, *others)
    above = rotated(last_row, "row", 1)
    product = first_product(part, below, rim, fronts)
    given, flipped = None, {}
    plan = {0: (2,), 1: (top, top - 1), 2: (1, 0)}
    for level in range(col_bits):
        if level == 1:
            product, above = tied(product, above)
        levels = plan.get(level, ())
        if levels:
            product, fronts_in = tied(product, fronts)
        got = swapped(product, "col", level)
        if levels:
            backs = turned(fronts_in, levels)
            got, first_back = tied(got, backs[0])
            backs = [first_back, *backs[1:]]
            flipped.update(zip(levels, backs))
        if level == 1:
            above = inner_only(above)
            got, above = tied(got, above)
        product, rim, given = next_product(level, col_bits, product, got, rim, given, fronts)
    arrays = (field, right_side, kappa, above, below, given)
    residual, at = None, 0

    def back_product(value, level):
        if level in flipped:
            return times_front(value, flipped[level])
        return times_front_t(value, fronts[level])

    def beside(step, value, residual, at, send):
        left = field.shape[0] - at
        share = left if step == -top else min(SHARES.get(step, 0), left)
        if not share:
            return send(value), residual, at
        value, *rest = tied(value, *arrays[:2], *([] if residual is None else [residual]))
        got = send(value)
        residual = stencil((*rest[:2], *arrays[2:]), rest[2] if rest[2:] else None, at, share)
        got, residual = tied(got, residual)
        return got, residual, at + share

    for level in range(col_bits, top + 1):
        axis, bit, owner = places[level]
        lower = jnp.bitwise_and(jnp.right_shift(owner, bit), 1) == 0
        got, residual, at = beside(
            level - top, product, residual, at, lambda v: swapped(v, axis, bit)
        )
        if level < top:
            state = jnp.where(lower, product + got, got - product)
            product = times_front(state, fronts[level + 1])
        else:
            state = back_product(got + got, level)
    for level in range(top - 1, -1, -1):
        axis, bit, owner = places[level]
        lower = jnp.bitwise_and(jnp.right_shift(owner, bit), 1) == 0
        got, residual, at = beside(
            level - top, state, residual, at, lambda v: swapped(v, axis, bit)
        )
        state = back_product(jnp.where(lower, state - got, state + got), level)
    return residual, state


SHARES = {0: 6, -2: 12, -3: 6}


def solution(mesh):
    placed = (P(None, "row", "col"), P(None, "row", "col"), P("row", "col"), P(None, "row", "col"))
    return jax.shard_map(
        body,
        mesh=mesh,
        in_specs=placed,
        out_specs=(P(None, "row", "col"), P("row", "col")),
        check_vma=False,
    )
```
